128 devices in a mesh: freq: 4 (over y), sky: 32 (over x, z, core).
Axes of the slice: x: 4, y: 4, z: 4, core: 2. Of those that a mesh axis runs over, the one named last changes fastest.
Arguments:
- stokes: bfloat16 [2, 288, 128, 1024], P(None, 'freq', 'sky'), may hold values from -48 to 48
- lam2: float32 [288], replicated, may hold values from 0.02 to 0.14
- peaks: int32 [8, 128, 1024], P(None, 'sky'), may hold values from 0 to 2047
- island_owner: int32 [1024, 1], P('sky'), may hold values from 0 to 31; in each aligned block of 32 rows (0 to 31, 32 to 63, ...) at most 2 rows name the same one
- fit_matrix: bfloat16 [32, 576, 512], P('sky', None, 'freq'), may hold values from -0.03125 to 0.03125
Outputs:
- residual_fdf: bfloat16 [2, 2048, 128, 1024], P(None, 'freq', 'sky')
- fit_coeffs: float32 [32, 32, 2, 128, 512], P('sky', None, None, None, 'freq')
The draws below stay inside these ranges and needn't reach their ends.
Inputs may be any that keep to these rules, and one draw needn't show every extreme that they name: `island_owner`: among the 32 blocks of one index of sky, no owner is named more than 2 times.
All inputs are finite; a program needn't handle non-finite values.
Results may differ from the reference program's by a relative error of at most 0.0065.
Values may be sent and summed in bfloat16 or wider, within the bound.
A program may use at most 192 MiB of HBM per device.

```python
import math
import jax
import jax.numpy as jnp
import numpy as np
from jax import lax

CH = 288
DEPTHS = 2048
K = 512
NCLEAN = 8
COLS = 1024
BLK = 128
ROWS = 128
NBLK = 32
BLOCKS = 1024
CAP = 2
OWNERS = 32
N_SKY = 32


def draw_peaks(key, part):
    key = jax.random.fold_in(key, 11)
    key_centre, key_offset, key_jump, key_which = jax.random.split(key, 4)
    shape = (NCLEAN, ROWS, COLS)
    centre = jax.random.randint(key_centre, (1, ROWS, COLS), 0, DEPTHS)
    offset = jax.random.randint(key_offset, shape, -3, 4)
    nearby = jnp.clip(centre + offset, 0, DEPTHS - 1)
    jumped = jax.random.randint(key_jump, shape, 0, DEPTHS)
    which = jax.random.randint(key_which, shape, 0, 8)
    return jnp.where(which == 0, jumped, nearby).astype(jnp.int32)


def level_of(key, shape, cuts, low, largest):
    level = 1.0
    for axis_at, blocks in cuts:
        draws = jax.random.uniform(jax.random.fold_in(jax.random.fold_in(key, 6), axis_at), (blocks,), jnp.float32, low / len(cuts), largest / len(cuts))
        level = level * jnp.repeat(jnp.exp(draws), shape[axis_at] // blocks).reshape((-1,) + (1,) * (len(shape) - 1 - axis_at))
    return level


def shared_out(stream_key, own, number, rows, number_of, top, limit, lean):
    ranking = jax.random.permutation(stream_key, number_of)
    heavy_load, ordinary = portions_of(number_of, rows * top, limit, lean, True), portions_of(number_of, rows * top, limit, lean, False)
    places = jnp.arange(number_of)

    def named(lengths, turn):
        used = int((lengths > 0).sum())
        fixed = max(1, used // 4)
        moved = fixed + (places - fixed + turn * (used - fixed)) % max(1, number_of - fixed)
        return jnp.zeros((number_of,), jnp.int32).at[ranking[jnp.where(places < fixed, places, moved)]].set(jnp.asarray(lengths, jnp.int32))

    lengths = jnp.where(number % 4 == 0, named(heavy_load, number // 4), named(ordinary, number - number // 4 - 1))
    mixed = jax.random.permutation(jax.random.fold_in(own, 3), number_of)
    source_of, receiver = mixed[0:number_of // 2 * 2:2], mixed[1:number_of // 2 * 2:2]
    room = jnp.minimum(lengths[source_of] - 1, limit - lengths[receiver]) // 2
    room = jnp.where((source_of == ranking[0]) | (receiver == ranking[0]) | (lengths[receiver] == 0), 0, jnp.maximum(room, 0))
    moved = jax.random.randint(jax.random.fold_in(own, 4), (number_of // 2,), 0, 1 << 20) % (room + 1)
    lengths = lengths.at[source_of].add(-moved).at[receiver].add(moved)
    items = jnp.searchsorted(jnp.cumsum(lengths), jnp.arange(rows * top), side="right").astype(jnp.int32)
    grid = items.reshape(top, rows).T
    grid = grid[jax.random.permutation(jax.random.fold_in(own, 1), rows)]
    turn = jax.random.randint(jax.random.fold_in(own, 2), (rows, 1), 0, top)
    return jnp.take_along_axis(grid, (jnp.arange(top)[None, :] + turn) % top, axis=1)


def portions_of(count, total, most, skew, full):
    loads = [(1 << 20) // math.isqrt(rank ** skew) + 1 for rank in range(1, count + 1)]
    largest = most if full else min(most, max(-(-total // count), total * loads[0] // sum(loads)))
    least = 1 if total - largest >= count - 1 else 0
    holding, rest = [largest] + [least] * (count - 1), total - largest - least * (count - 1)
    while rest > 0:
        free = [i for i in range(1, count) if holding[i] < largest] or [i for i in range(1, count) if holding[i] < most]
        mass, left = sum([loads[i] for i in free]), rest
        for i in free:
            more = min(most - holding[i], max(1, left * loads[i] // mass), rest)
            holding[i] = holding[i] + more
            rest = rest - more
    return np.array(holding)


def noise(own_key, extent, scale, limit, shards=(), kind=jnp.bfloat16):
    entries = scale * jax.random.normal(own_key, extent, jnp.float32)
    if shards:
        entries = entries * level_of(own_key, extent, shards, -0.22, 0.18)
    return jnp.clip(entries, -limit, limit).astype(kind)


def setup_inputs(seed: int = 0) -> dict:
    key_list = jax.random.split(jax.random.key(seed), 6)
    stokes = noise(key_list[0], (2, CH, ROWS, COLS), 8.0, 48.0, ((1, 4), (2, 32)))
    lam2 = jnp.clip(jnp.exp(jax.random.uniform(key_list[1], (CH,), jnp.float32, math.log(0.02), math.log(0.14))), 0.02, 0.14)
    peaks = draw_peaks(jax.random.fold_in(key_list[5], 71), 0)
    island_owner_keys = jax.random.split(jax.random.fold_in(key_list[3], 1), BLOCKS // NBLK)
    island_owner_turns = jax.random.permutation(jax.random.fold_in(key_list[3], 3), BLOCKS // NBLK)
    island_owner = jax.vmap(lambda own, number: shared_out(jax.random.fold_in(key_list[3], 2), own, number, NBLK, N_SKY, 1, CAP, 2))(island_owner_keys, island_owner_turns).reshape((BLOCKS, 1))
    fit_matrix = noise(key_list[4], (OWNERS, 2 * CH, K), (128 * CH) ** -0.5, 0.03125, ((0, 32), (2, 4)))
    return dict(stokes=stokes, lam2=lam2, peaks=peaks, island_owner=island_owner, fit_matrix=fit_matrix)


DEPTH_STEP = 2.5
CLEAN_GAIN = 0.3


def peak_values(spectra, offsets, depth_values):
    results = []
    for current in range(depth_values.shape[0]):
        angles = 2.0 * offsets[:, None] * depth_values[current][None, :]
        cosine = jnp.cos(angles)
        sine_part = jnp.sin(angles)
        real_part = jnp.sum(spectra[0] * cosine + spectra[1] * sine_part, axis=0)
        imag_part = jnp.sum(spectra[1] * cosine - spectra[0] * sine_part, axis=0)
        results.append(jnp.stack([real_part, imag_part]))
    return jnp.stack(results)


def spread_table(offsets, depth_total):
    shifts = (jnp.arange(2 * depth_total - 1) - (depth_total - 1)).astype(offsets.dtype) * DEPTH_STEP
    angles = 2.0 * offsets[:, None] * shifts[None, :]
    stacked = jnp.stack([jnp.sum(jnp.cos(angles), axis=0), -jnp.sum(jnp.sin(angles), axis=0)])
    return stacked / offsets.shape[0]


def clean_components(values, picks, spread, depth_total):
    components = []
    for current in range(values.shape[0]):
        value_real = values[current, 0]
        value_imag = values[current, 1]
        for earlier in range(current):
            lookup = (picks[current] - picks[earlier] + depth_total - 1).astype(jnp.int32)
            spread_real = jnp.take(spread[0], lookup)
            spread_imag = jnp.take(spread[1], lookup)
            comp_real, comp_imag = components[earlier]
            value_real = value_real - (comp_real * spread_real - comp_imag * spread_imag)
            value_imag = value_imag - (comp_real * spread_imag + comp_imag * spread_real)
        components.append((CLEAN_GAIN * value_real, CLEAN_GAIN * value_imag))
    return components


def subtract_model(spectra, offsets, depth_values, components):
    model_real = jnp.zeros_like(spectra[0])
    model_imag = jnp.zeros_like(spectra[0])
    for current in range(depth_values.shape[0]):
        angles = 2.0 * offsets[:, None] * depth_values[current][None, :]
        cosine = jnp.cos(angles)
        sine_part = jnp.sin(angles)
        comp_real, comp_imag = components[current]
        model_real = model_real + (comp_real[None, :] * cosine - comp_imag[None, :] * sine_part)
        model_imag = model_imag + (comp_real[None, :] * sine_part + comp_imag[None, :] * cosine)
    return jnp.stack([spectra[0] - model_real, spectra[1] - model_imag]).astype(jnp.bfloat16)


def synthesis_kernel(offsets, first_depth, count):
    depth_ids = (jnp.arange(count) + first_depth - DEPTHS // 2).astype(offsets.dtype) * DEPTH_STEP
    angles = 2.0 * offsets[:, None] * depth_ids[None, :]
    cosine = jnp.cos(angles)
    sine_part = jnp.sin(angles)
    rows_stokes_q = jnp.concatenate([cosine, -sine_part], axis=1)
    rows_stokes_u = jnp.concatenate([sine_part, cosine], axis=1)
    return (jnp.concatenate([rows_stokes_q, rows_stokes_u], axis=0) / offsets.shape[0]).astype(jnp.bfloat16)


def slot_blocks(blocks, owners, owner_count, capacity):
    block_count = owners.shape[0]
    onehot = (owners[:, None] == jnp.arange(owner_count)[None, :]).astype(jnp.int32)
    slot_rank = jnp.sum((jnp.cumsum(onehot, axis=0) - onehot) * onehot, axis=1)
    matches = (owners[None, None, :] == jnp.arange(owner_count)[:, None, None]) & (
        slot_rank[None, None, :] == jnp.arange(capacity)[None, :, None])
    chosen = jnp.sum(jnp.where(matches, jnp.arange(block_count)[None, None, :], 0), axis=2).astype(jnp.int32)
    filled = jnp.any(matches, axis=2)
    picked = jnp.take(blocks, chosen.reshape(-1), axis=0)
    picked = picked.reshape((owner_count, capacity) + blocks.shape[1:])
    return jnp.where(filled[:, :, None, None], picked, jnp.zeros_like(picked))


def reference(stokes, lam2, peaks, island_owner, fit_matrix):
    offsets = lam2 - jnp.mean(lam2)
    pixels = ROWS * COLS
    spectra = stokes.astype(jnp.float32).reshape(2, CH, pixels)
    picks = peaks.reshape(NCLEAN, pixels)
    depth_values = (picks - DEPTHS // 2).astype(jnp.float32) * DEPTH_STEP
    values = peak_values(spectra, offsets, depth_values) / CH
    spread = spread_table(offsets, DEPTHS)
    components = clean_components(values, picks, spread, DEPTHS)
    residual = subtract_model(spectra, offsets, depth_values, components)
    kernel = synthesis_kernel(offsets, 0, DEPTHS).astype(jnp.float32)
    planes = jnp.transpose(residual.reshape(2 * CH, ROWS, COLS), (1, 0, 2))

    def one_row(plane):
        product = jnp.dot(kernel.T, plane.astype(jnp.float32), preferred_element_type=jnp.float32)
        return product.astype(jnp.bfloat16)

    rows_out = lax.map(one_row, planes)
    residual_fdf = jnp.transpose(rows_out.reshape(ROWS, 2, DEPTHS, COLS), (1, 2, 0, 3))
    pixel_rows = residual.reshape(2 * CH, pixels).T
    blocks = pixel_rows.reshape(N_SKY, NBLK, BLK, 2 * CH)
    owners = island_owner.reshape(N_SKY, NBLK)

    def source_slots(source_blocks, source_owners):
        return slot_blocks(source_blocks, source_owners, N_SKY, CAP)

    slots = jax.vmap(source_slots)(blocks, owners)
    by_owner = jnp.swapaxes(slots, 0, 1)

    def fit_owner(pair):
        owner_slots, matrix = pair
        return jnp.einsum("snpv,vk->snpk", owner_slots.astype(jnp.float32), matrix.astype(jnp.float32))

    fit_coeffs = lax.map(fit_owner, (by_owner, fit_matrix))
    return residual_fdf, fit_coeffs
```

```python
import functools
import jax
import jax.numpy as jnp
from jax import lax
from jax.sharding import PartitionSpec as P
from jax.experimental import pallas as pl
from jax.experimental.pallas import tpu as pltpu

NC = 8
DEPTHS = 2048
STEP = 2.5
BLK = 128
GAIN = 0.3
LOW = 64
HIGH = 32

def gather(x, idx):
    return jnp.take_along_axis(x, idx, axis=1, mode="promise_in_bounds")

def full(row):
    return jnp.broadcast_to(row, (8, 128))

def clean_tile(groups, chans, data_ref, picks, t_ref, r_ref, out_ref, oh, e4, ec, es):
    lo = picks & (LOW - 1)
    hi = picks >> 6
    for j in range(NC):
        cols = slice(j * 128, (j + 1) * 128)
        low = (lax.broadcasted_iota(jnp.int32, (LOW, 128), 0) == lo[j:j+1]).astype(jnp.bfloat16)
        high = (lax.broadcasted_iota(jnp.int32, (HIGH, 128), 0) == hi[j:j+1]).astype(jnp.bfloat16)
        oh[0:LOW, cols] = low
        oh[LOW:2*LOW, cols] = low
        oh[2*LOW:2*LOW+HIGH, cols] = high
        oh[2*LOW+HIGH:, cols] = high
    e4[...] = jnp.dot(t_ref[...], oh[...], preferred_element_type=jnp.float32)

    def peak(g, acc):
        x = data_ref[pl.ds(pl.multiple_of(g * 16, 16), 16), :].astype(jnp.float32)
        q, u = x[:8], x[8:]
        base = pl.multiple_of(g * 32, 32)
        out = []
        for j in range(NC):
            cols = slice(j * 128, (j + 1) * 128)
            cl, sl = e4[pl.ds(base, 8), cols], e4[pl.ds(base + 8, 8), cols]
            ch, sh = e4[pl.ds(base + 16, 8), cols], e4[pl.ds(base + 24, 8), cols]
            c = ch * cl - sh * sl
            s = sh * cl + ch * sl
            ec[g * NC + j] = c
            es[g * NC + j] = s
            out.append((acc[j][0] + (q * c + u * s), acc[j][1] + (u * c - q * s)))
        return tuple(out)

    zero = jnp.zeros((8, 128), jnp.float32)
    acc = lax.fori_loop(0, groups, peak, tuple((zero, zero) for _ in range(NC)))
    scale = 1.0 / chans
    vr = jnp.concatenate([jnp.sum(a[0], axis=0, keepdims=True) for a in acc], axis=0) * scale
    vi = jnp.concatenate([jnp.sum(a[1], axis=0, keepdims=True) for a in acc], axis=0) * scale
    comps = []
    for i in range(NC):
        cr = full(vr[i:i+1] * GAIN)
        ci = full(vi[i:i+1] * GAIN)
        comps.append((cr, ci))
        if i == NC - 1:
            break
        d = picks - picks[i:i+1]
        a = jnp.abs(d)
        alo, ahi = a & 127, a >> 7
        rr, ri = zero, zero
        for h in range(16):
            here = ahi == h
            rr = jnp.where(here, gather(full(r_ref[0, h:h+1, :]), alo), rr)
            ri = jnp.where(here, gather(full(r_ref[1, h:h+1, :]), alo), ri)
        ri = jnp.where(d < 0, -ri, ri)
        vr = vr - (cr * rr - ci * ri)
        vi = vi - (cr * ri + ci * rr)

    def model(g, _):
        rows16 = pl.ds(pl.multiple_of(g * 16, 16), 16)
        x = data_ref[rows16, :].astype(jnp.float32)
        mr, mi = zero, zero
        for j in range(NC):
            c, s = ec[g * NC + j], es[g * NC + j]
            cr, ci = comps[j]
            mr = mr + (cr * c - ci * s)
            mi = mi + (cr * s + ci * c)
        out_ref[rows16, :] = jnp.concatenate([x[:8] - mr, x[8:] - mi], axis=0).astype(jnp.bfloat16)
        return 0

    lax.fori_loop(0, groups, model, 0)

def kernel(groups, chans, data_ref, picks_ref, t_ref, r_ref, out_ref, oh, e4, ec, es):
    clean_tile(groups, chans, data_ref, picks_ref[...], t_ref, r_ref, out_ref, oh, e4, ec, es)

def clean(data, picks, t, r, chans):
    groups = chans // 8
    pixels = data.shape[1]
    return pl.pallas_call(
        functools.partial(kernel, groups, chans),
        grid=(pixels // 128,),
        in_specs=[
            pl.BlockSpec((2 * chans, 128), lambda i: (0, i)),
            pl.BlockSpec((NC, 128), lambda i: (0, i)),
            pl.BlockSpec((4 * chans, 2 * (LOW + HIGH)), lambda i: (0, 0)),
            pl.BlockSpec((2, 16, 128), lambda i: (0, 0, 0)),
        ],
        out_specs=pl.BlockSpec((2 * chans, 128), lambda i: (0, i)),
        out_shape=jax.ShapeDtypeStruct((2 * chans, pixels), jnp.bfloat16),
        scratch_shapes=[pltpu.VMEM((2 * (LOW + HIGH), 1024), jnp.bfloat16), pltpu.VMEM((4 * chans, 1024), jnp.float32)] + [pltpu.VMEM((groups * NC, 8, 128), jnp.float32)] * 2,
        compiler_params=pltpu.CompilerParams(vmem_limit_bytes=40 << 20),
        name="clean",
    )(data, picks, t, r)

def split(x):
    top = lax.reduce_precision(x, 8, 7)
    return top, x - top

def tables(lam2):
    chans = lam2.shape[0]
    off = lam2 - jnp.mean(lam2)
    a2 = 2.0 * off
    lo = a2[:, None] * (jnp.arange(LOW, dtype=jnp.float32) * 2.5)[None]
    hi = a2[:, None] * ((jnp.arange(HIGH, dtype=jnp.float32) * LOW - 1024.0) * 2.5)[None]
    def rows(a):
        return jnp.stack([jnp.cos(a), jnp.sin(a)]).reshape(2, chans // 8, 8, -1)
    l1, l2 = split(rows(lo)); h1, h2 = split(rows(hi))
    zl, zh = jnp.zeros_like(l1), jnp.zeros_like(h1)
    low = jnp.concatenate([l1, l2, zh, zh], -1)
    high = jnp.concatenate([zl, zl, h1, h2], -1)
    t = jnp.transpose(jnp.concatenate([low, high], 0), (1, 0, 2, 3)).reshape(4 * chans, -1)
    return off, t.astype(jnp.bfloat16)

def spread(off):
    a2 = 2.0 * off
    ah = (jnp.arange(16, dtype=jnp.float32) * 320.0)[:, None] * a2[None, :]
    ca, sa = jnp.cos(ah), jnp.sin(ah)
    al = a2[:, None] * (jnp.arange(128, dtype=jnp.float32) * 2.5)[None]
    left = jnp.stack([jnp.concatenate([ca, -sa], 1), jnp.concatenate([-sa, -ca], 1)])
    right = jnp.concatenate([jnp.cos(al), jnp.sin(al)], 0)
    return jnp.einsum("ahc,cl->ahl", left, right, precision=lax.Precision.HIGHEST) / off.shape[0]


def synthesis(off, first, count):
    chans = off.shape[0]
    per_row = jnp.broadcast_to(off.reshape(chans // 8, 1, 8), (chans // 8, 2, 8)).reshape(1, 2 * chans)
    is_u = (lax.broadcasted_iota(jnp.int32, (1, 2 * chans), 1) // 8) % 2 == 1
    depth = (jnp.arange(count) + first - DEPTHS // 2).astype(jnp.float32) * STEP
    angle = (2.0 * per_row) * depth[:, None]
    cosine, sine = jnp.cos(angle), jnp.sin(angle)
    real = jnp.where(is_u, sine, cosine)
    imag = jnp.where(is_u, cosine, -sine)
    return (jnp.concatenate([real, imag], axis=0) / chans).astype(jnp.bfloat16)


def fdf_kernel(k_ref, res_ref, out_ref, mixed):
    rows, depths, width = res_ref.shape[0], k_ref.shape[0], res_ref.shape[2]
    for row in range(rows):
        for first in range(0, depths, 256):
            part = jnp.dot(k_ref[first:first + 256, :], res_ref[row], preferred_element_type=jnp.float32)
            for c in range(width // 128):
                mixed[c, pl.ds(first * rows + row, 256, rows), :] = part[:, c * 128:(c + 1) * 128]
    for c in range(width // 128):
        block = mixed[c].astype(jnp.bfloat16)
        out_ref[:, :, :, c * 128:(c + 1) * 128] = block.reshape(2, depths // 2, rows, 128)


def fdf(kt, res):
    rows, total, columns = res.shape
    depths = kt.shape[0]
    width = 256
    return pl.pallas_call(
        fdf_kernel,
        grid=(columns // width,),
        in_specs=[
            pl.BlockSpec((depths, total), lambda i: (0, 0)),
            pl.BlockSpec((rows, total, width), lambda i: (0, 0, i)),
        ],
        out_specs=pl.BlockSpec((2, depths // 2, rows, width), lambda i: (0, 0, 0, i)),
        out_shape=jax.ShapeDtypeStruct((2, depths // 2, rows, columns), jnp.bfloat16),
        scratch_shapes=[pltpu.VMEM((width // 128, depths * rows, 128), jnp.float32)],
        compiler_params=pltpu.CompilerParams(vmem_limit_bytes=48 << 20),
        cost_estimate=pl.CostEstimate(flops=2 * depths * total * rows * columns, bytes_accessed=14 << 20, transcendentals=0),
        name="fdf",
    )(kt, res)


def slots_of(owners, count, capacity):
    blocks = owners.shape[0]
    index = jnp.arange(blocks)
    earlier = (owners[:, None] == owners[None, :]) & (index[None, :] < index[:, None])
    rank = jnp.sum(earlier.astype(jnp.int32), axis=1)
    hit = (owners[None, None, :] == jnp.arange(count)[:, None, None]) & (
        rank[None, None, :] == jnp.arange(capacity)[None, :, None])
    chosen = jnp.sum(jnp.where(hit, index[None, None, :], 0), axis=2).astype(jnp.int32)
    filled = jnp.sum(hit.astype(jnp.int32), axis=2)
    return chosen, filled


def fit_kernel(chosen, filled, *refs):
    capacity = len(refs) - 2
    w_ref, out_ref = refs[-2], refs[-1]
    owner = pl.program_id(0)
    for rank in range(capacity):
        value = lax.dot_general(refs[rank][0], w_ref[0], (((0,), (0,)), ((), ())), preferred_element_type=jnp.float32)
        out_ref[0, rank] = jnp.where(filled[owner, rank] > 0, value, 0.0).astype(jnp.bfloat16)


def fits(chosen, filled, res, w):
    count, capacity = chosen.shape
    rows, total, columns = res.shape
    per_row = columns // BLK
    terms = w.shape[2]

    def pick(rank):
        return pl.BlockSpec((1, total, BLK), lambda o, c, f: (c[o, rank] // per_row, 0, c[o, rank] % per_row))

    return pl.pallas_call(
        fit_kernel,
        grid_spec=pltpu.PrefetchScalarGridSpec(
            num_scalar_prefetch=2,
            grid=(count,),
            in_specs=[pick(rank) for rank in range(capacity)] + [pl.BlockSpec((1, total, terms), lambda o, c, f: (o, 0, 0))],
            out_specs=pl.BlockSpec((1, capacity, BLK, terms), lambda o, c, f: (o, 0, 0, 0)),
        ),
        out_shape=jax.ShapeDtypeStruct((count, capacity, BLK, terms), jnp.bfloat16),
        compiler_params=pltpu.CompilerParams(vmem_limit_bytes=32 << 20),
        name="fits",
    )(chosen, filled, *([res] * capacity), w)


def grouped(x, chans):
    tail = x.shape[2:]
    return jnp.swapaxes(x.reshape((2, chans // 8, 8) + tail), 0, 1)


def shards(stokes, lam2, peaks, island_owner, fit_matrix):
    freq = lax.axis_index("freq")
    freq_count, sky_count = lax.axis_size("freq"), lax.axis_size("sky")
    chans, local = lam2.shape[0], stokes.shape[1]
    rows, columns = stokes.shape[2], stokes.shape[3]
    capacity = max(2, 2 * island_owner.shape[0] // sky_count)
    weights = grouped(fit_matrix[0].reshape(2, chans, -1), chans).reshape(2 * chans, -1)
    weights = lax.all_gather(weights, "sky", axis=0)
    off, t = tables(lam2)
    outgoing = jnp.moveaxis(grouped(stokes, local), 3, 0).reshape(rows, 2 * local, columns)
    data = lax.all_to_all(outgoing, "freq", split_axis=0, concat_axis=0, tiled=True)
    picks = lax.dynamic_index_in_dim(peaks, freq, 1, keepdims=False)
    res = clean(data.reshape(2 * chans, columns), picks, t, spread(off), chans)
    res = lax.all_gather(res, "freq", axis=0)
    depths = DEPTHS // freq_count
    kt = synthesis(off, freq * depths, depths)
    chosen, filled = slots_of(island_owner[:, 0], sky_count, capacity)
    sent = fits(chosen, filled, res, weights)
    got = lax.all_to_all(sent, "sky", split_axis=0, concat_axis=0, tiled=True)
    return fdf(kt, res), got.astype(jnp.float32)[None]


def solution(mesh):
    in_specs = (
        P(None, "freq", "sky", None),
        P(),
        P(None, "sky", None),
        P("sky", None),
        P("sky", None, "freq"),
    )
    out_specs = (P(None, "freq", "sky", None), P("sky", None, None, None, "freq"))
    return jax.shard_map(shards, mesh=mesh, in_specs=in_specs, out_specs=out_specs, check_vma=False)
```

```python
import functools
import jax
import jax.numpy as jnp
from jax import lax
from jax.sharding import PartitionSpec as P
from jax.experimental import pallas as pl
from jax.experimental.pallas import tpu as pltpu

NC = 8
DEPTHS = 2048
STEP = 2.5
BLK = 128
LAG = 2
MESH = pl.DeviceIdType.MESH
GAIN = 0.3
LOW = 64
HIGH = 32

def gather(x, idx):
    return jnp.take_along_axis(x, idx, axis=1, mode="promise_in_bounds")

def full(row):
    return jnp.broadcast_to(row, (8, 128))

def clean_tile(groups, chans, data_ref, picks, t_ref, r_ref, out_ref, oh, e4, ec, es):
    per = data_ref.shape[1] // 16
    lo = picks & (LOW - 1)
    hi = picks >> 6
    for j in range(NC):
        cols = slice(j * 128, (j + 1) * 128)
        low = (lax.broadcasted_iota(jnp.int32, (LOW, 128), 0) == lo[j:j+1]).astype(jnp.bfloat16)
        high = (lax.broadcasted_iota(jnp.int32, (HIGH, 128), 0) == hi[j:j+1]).astype(jnp.bfloat16)
        oh[0:LOW, cols] = low
        oh[LOW:2*LOW, cols] = low
        oh[2*LOW:2*LOW+HIGH, cols] = high
        oh[2*LOW+HIGH:, cols] = high
    e4[...] = jnp.dot(t_ref[...], oh[...], preferred_element_type=jnp.float32)

    def peak(g, acc):
        x = data_ref[g // per, pl.ds(pl.multiple_of(g % per * 16, 16), 16), :].astype(jnp.float32)
        q, u = x[:8], x[8:]
        base = pl.multiple_of(g * 32, 32)
        out = []
        for j in range(NC):
            cols = slice(j * 128, (j + 1) * 128)
            cl, sl = e4[pl.ds(base, 8), cols], e4[pl.ds(base + 8, 8), cols]
            ch, sh = e4[pl.ds(base + 16, 8), cols], e4[pl.ds(base + 24, 8), cols]
            c = ch * cl - sh * sl
            s = sh * cl + ch * sl
            ec[g * NC + j] = c
            es[g * NC + j] = s
            out.append((acc[j][0] + (q * c + u * s), acc[j][1] + (u * c - q * s)))
        return tuple(out)

    zero = jnp.zeros((8, 128), jnp.float32)
    acc = lax.fori_loop(0, groups, peak, tuple((zero, zero) for _ in range(NC)))
    scale = 1.0 / chans
    vr = jnp.concatenate([jnp.sum(a[0], axis=0, keepdims=True) for a in acc], axis=0) * scale
    vi = jnp.concatenate([jnp.sum(a[1], axis=0, keepdims=True) for a in acc], axis=0) * scale
    comps = []
    for i in range(NC):
        cr = full(vr[i:i+1] * GAIN)
        ci = full(vi[i:i+1] * GAIN)
        comps.append((cr, ci))
        if i == NC - 1:
            break
        d = picks - picks[i:i+1]
        a = jnp.abs(d)
        alo, ahi = a & 127, a >> 7
        rr, ri = zero, zero
        for h in range(16):
            here = ahi == h
            rr = jnp.where(here, gather(full(r_ref[0, h:h+1, :]), alo), rr)
            ri = jnp.where(here, gather(full(r_ref[1, h:h+1, :]), alo), ri)
        ri = jnp.where(d < 0, -ri, ri)
        vr = vr - (cr * rr - ci * ri)
        vi = vi - (cr * ri + ci * rr)

    def model(g, _):
        rows16 = pl.ds(pl.multiple_of(g * 16, 16), 16)
        x = data_ref[g // per, pl.ds(pl.multiple_of(g % per * 16, 16), 16), :].astype(jnp.float32)
        mr, mi = zero, zero
        for j in range(NC):
            c, s = ec[g * NC + j], es[g * NC + j]
            cr, ci = comps[j]
            mr = mr + (cr * c - ci * s)
            mi = mi + (cr * s + ci * c)
        out_ref[rows16, :] = jnp.concatenate([x[:8] - mr, x[8:] - mi], axis=0).astype(jnp.bfloat16)
        return 0

    lax.fori_loop(0, groups, model, 0)

def gather_kernel(groups, chans, send_ref, picks_ref, t_ref, r_ref, out_ref, data, res, oh, e4, ec, es, own, sa, ra, sn, rn, sf, rf, so):
    count = lax.axis_size("freq")
    me = lax.axis_index("freq")
    chunks = picks_ref.shape[0]
    half = chans
    to_right = {"freq": lax.rem(me + 1, count)}
    to_left = {"freq": lax.rem(me + count - 1, count)}
    left = lax.rem(me + count - 1, count)
    right = lax.rem(me + 1, count)
    far = lax.rem(me + 2, count)

    barrier = pltpu.get_barrier_semaphore()
    for k in range(1, count):
        pl.semaphore_signal(barrier, inc=1, device_id={"freq": lax.rem(me + k, count)}, device_id_type=MESH)
    pl.semaphore_wait(barrier, count - 1)

    def part(c, k):
        peer = lax.rem(me + k, count)
        return pltpu.make_async_remote_copy(
            src_ref=send_ref.at[peer, c], dst_ref=data.at[c, me],
            send_sem=sa.at[c, k], recv_sem=ra.at[c, k], device_id={"freq": peer}, device_id_type=MESH)

    def arrived(c, k):
        source = lax.rem(me + count - k, count)
        return pltpu.make_async_remote_copy(
            src_ref=send_ref.at[source, c], dst_ref=data.at[c, source],
            send_sem=sa.at[c, k], recv_sem=ra.at[c, k], device_id={"freq": source}, device_id_type=MESH)

    def kept(c):
        return pltpu.make_async_copy(send_ref.at[me, c], data.at[c, me], own.at[c])

    def start_parts(c, _):
        kept(c).start()
        for k in (1, 3, 2):
            part(c, k).start()
        return 0

    lax.fori_loop(0, chunks, start_parts, 0)

    def to_neighbour(c, way, source):
        return pltpu.make_async_remote_copy(
            src_ref=res.at[source, c], dst_ref=res.at[source, c],
            send_sem=sn.at[c, way], recv_sem=rn.at[c, way],
            device_id=to_right if way == 0 else to_left, device_id_type=MESH)

    def onward(c, way, source):
        rows = pl.ds(way * half, half)
        return pltpu.make_async_remote_copy(
            src_ref=res.at[source, c, rows], dst_ref=res.at[source, c, rows],
            send_sem=sf.at[c, way], recv_sem=rf.at[c, way],
            device_id=to_right if way == 0 else to_left, device_id_type=MESH)

    def keep(c, source):
        return pltpu.make_async_copy(res.at[source, c], out_ref.at[source, c], so.at[c, source])

    def relay(c):
        to_neighbour(c, 0, left).wait_recv()
        onward(c, 0, left).start()
        keep(c, left).start()
        to_neighbour(c, 1, right).wait_recv()
        onward(c, 1, right).start()
        keep(c, right).start()

    def step(c, _):
        kept(c).wait()
        for k in (1, 3, 2):
            arrived(c, k).wait_recv()
        clean_tile(groups, chans, data.at[c], picks_ref[c], t_ref, r_ref, res.at[me, c], oh, e4, ec, es)
        to_neighbour(c, 0, me).start()
        to_neighbour(c, 1, me).start()
        keep(c, me).start()

        @pl.when(c >= LAG)
        def _():
            relay(c - LAG)
        return 0

    lax.fori_loop(0, chunks, step, 0)
    for c in range(chunks - LAG, chunks):
        relay(c)

    def finish(c, _):
        onward(c, 0, far).wait_recv()
        onward(c, 1, far).wait_recv()
        keep(c, far).start()
        for k in (1, 3, 2):
            part(c, k).wait_send()
        to_neighbour(c, 0, me).wait_send()
        to_neighbour(c, 1, me).wait_send()
        onward(c, 0, left).wait_send()
        onward(c, 1, right).wait_send()
        return 0

    lax.fori_loop(0, chunks, finish, 0)

    def written(c, _):
        for source in (me, left, right, far):
            keep(c, source).wait()
        return 0

    lax.fori_loop(0, chunks, written, 0)


def clean_gather(send, picks, t, r, chans):
    groups = chans // 8
    count, chunks, local, width = send.shape
    dma = pltpu.SemaphoreType.DMA
    vmem = pl.BlockSpec(memory_space=pltpu.VMEM)
    return pl.pallas_call(
        functools.partial(gather_kernel, groups, chans),
        in_specs=[vmem] * 4,
        out_specs=pl.BlockSpec(memory_space=pl.ANY),
        out_shape=jax.ShapeDtypeStruct((count, chunks, 2 * chans, width), jnp.bfloat16),
        scratch_shapes=[
            pltpu.VMEM((chunks, count, local, width), jnp.bfloat16),
            pltpu.VMEM((count, chunks, 2 * chans, width), jnp.bfloat16),
            pltpu.VMEM((2 * (LOW + HIGH), NC * width), jnp.bfloat16),
            pltpu.VMEM((4 * chans, NC * width), jnp.float32),
            pltpu.VMEM((groups * NC, 8, width), jnp.float32),
            pltpu.VMEM((groups * NC, 8, width), jnp.float32),
            dma((chunks,)), dma((chunks, count)), dma((chunks, count)),
            dma((chunks, 2)), dma((chunks, 2)), dma((chunks, 2)), dma((chunks, 2)), dma((chunks, count)),
        ],
        compiler_params=pltpu.CompilerParams(collective_id=0, has_side_effects=True, vmem_limit_bytes=48 << 20),
        cost_estimate=pl.CostEstimate(flops=3 << 32, bytes_accessed=16 << 20, transcendentals=0),
        name="clean_gather",
    )(send, picks, t, r)


def split(x):
    top = lax.reduce_precision(x, 8, 7)
    return top, x - top

def tables(lam2):
    chans = lam2.shape[0]
    off = lam2 - jnp.mean(lam2)
    a2 = 2.0 * off
    lo = a2[:, None] * (jnp.arange(LOW, dtype=jnp.float32) * 2.5)[None]
    hi = a2[:, None] * ((jnp.arange(HIGH, dtype=jnp.float32) * LOW - 1024.0) * 2.5)[None]
    def rows(a):
        return jnp.stack([jnp.cos(a), jnp.sin(a)]).reshape(2, chans // 8, 8, -1)
    l1, l2 = split(rows(lo)); h1, h2 = split(rows(hi))
    zl, zh = jnp.zeros_like(l1), jnp.zeros_like(h1)
    low = jnp.concatenate([l1, l2, zh, zh], -1)
    high = jnp.concatenate([zl, zl, h1, h2], -1)
    t = jnp.transpose(jnp.concatenate([low, high], 0), (1, 0, 2, 3)).reshape(4 * chans, -1)
    return off, t.astype(jnp.bfloat16)

def spread(off):
    a2 = 2.0 * off
    ah = (jnp.arange(16, dtype=jnp.float32) * 320.0)[:, None] * a2[None, :]
    ca, sa = jnp.cos(ah), jnp.sin(ah)
    al = a2[:, None] * (jnp.arange(128, dtype=jnp.float32) * 2.5)[None]
    left = jnp.stack([jnp.concatenate([ca, -sa], 1), jnp.concatenate([-sa, -ca], 1)])
    right = jnp.concatenate([jnp.cos(al), jnp.sin(al)], 0)
    return jnp.einsum("ahc,cl->ahl", left, right, precision=lax.Precision.HIGHEST) / off.shape[0]


def synthesis(off, first, count):
    chans = off.shape[0]
    per_row = jnp.broadcast_to(off.reshape(chans // 8, 1, 8), (chans // 8, 2, 8)).reshape(1, 2 * chans)
    is_u = (lax.broadcasted_iota(jnp.int32, (1, 2 * chans), 1) // 8) % 2 == 1
    depth = (jnp.arange(count) + first - DEPTHS // 2).astype(jnp.float32) * STEP
    angle = (2.0 * per_row) * depth[:, None]
    cosine, sine = jnp.cos(angle), jnp.sin(angle)
    real = jnp.where(is_u, sine, cosine)
    imag = jnp.where(is_u, cosine, -sine)
    return (jnp.concatenate([real, imag], axis=0) / chans).astype(jnp.bfloat16)


def fdf_kernel(k_ref, res_ref, out_ref, mixed):
    rows, depths, width = res_ref.shape[0], k_ref.shape[0], res_ref.shape[1] * 128
    for row in range(rows):
        block = jnp.concatenate([res_ref[row, c] for c in range(width // 128)], axis=1)
        for first in range(0, depths, 256):
            part = jnp.dot(k_ref[first:first + 256, :], block, preferred_element_type=jnp.float32)
            for c in range(width // 128):
                mixed[c, pl.ds(first * rows + row, 256, rows), :] = part[:, c * 128:(c + 1) * 128]
    for c in range(width // 128):
        block = mixed[c].astype(jnp.bfloat16)
        out_ref[:, :, :, c * 128:(c + 1) * 128] = block.reshape(2, depths // 2, rows, 128)


def fdf(kt, res):
    rows, chunks, total, _ = res.shape
    columns = chunks * 128
    depths = kt.shape[0]
    width = 256
    return pl.pallas_call(
        fdf_kernel,
        grid=(columns // width,),
        in_specs=[
            pl.BlockSpec((depths, total), lambda i: (0, 0)),
            pl.BlockSpec((rows, width // 128, total, 128), lambda i: (0, i, 0, 0)),
        ],
        out_specs=pl.BlockSpec((2, depths // 2, rows, width), lambda i: (0, 0, 0, i)),
        out_shape=jax.ShapeDtypeStruct((2, depths // 2, rows, columns), jnp.bfloat16),
        scratch_shapes=[pltpu.VMEM((width // 128, depths * rows, 128), jnp.float32)],
        compiler_params=pltpu.CompilerParams(vmem_limit_bytes=48 << 20),
        cost_estimate=pl.CostEstimate(flops=2 * depths * total * rows * columns, bytes_accessed=14 << 20, transcendentals=0),
        name="fdf",
    )(kt, res)


def slots_of(owners, count, capacity):
    blocks = owners.shape[0]
    index = jnp.arange(blocks)
    earlier = (owners[:, None] == owners[None, :]) & (index[None, :] < index[:, None])
    rank = jnp.sum(earlier.astype(jnp.int32), axis=1)
    hit = (owners[None, None, :] == jnp.arange(count)[:, None, None]) & (
        rank[None, None, :] == jnp.arange(capacity)[None, :, None])
    chosen = jnp.sum(jnp.where(hit, index[None, None, :], 0), axis=2).astype(jnp.int32)
    filled = jnp.sum(hit.astype(jnp.int32), axis=2)
    return chosen, filled


def fit_kernel(chosen, filled, *refs):
    capacity = len(refs) - 2
    w_ref, out_ref = refs[-2], refs[-1]
    owner = pl.program_id(0)
    for rank in range(capacity):
        value = lax.dot_general(refs[rank][0, 0], w_ref[0], (((0,), (0,)), ((), ())), preferred_element_type=jnp.float32)
        out_ref[0, rank] = jnp.where(filled[owner, rank] > 0, value, 0.0).astype(jnp.bfloat16)


def fits(chosen, filled, res, w):
    count, capacity = chosen.shape
    _, per_row, total, _ = res.shape
    terms = w.shape[2]

    def pick(rank):
        return pl.BlockSpec((1, 1, total, BLK), lambda o, c, f: (c[o, rank] // per_row, c[o, rank] % per_row, 0, 0))

    return pl.pallas_call(
        fit_kernel,
        grid_spec=pltpu.PrefetchScalarGridSpec(
            num_scalar_prefetch=2,
            grid=(count,),
            in_specs=[pick(rank) for rank in range(capacity)] + [pl.BlockSpec((1, total, terms), lambda o, c, f: (o, 0, 0))],
            out_specs=pl.BlockSpec((1, capacity, BLK, terms), lambda o, c, f: (o, 0, 0, 0)),
        ),
        out_shape=jax.ShapeDtypeStruct((count, capacity, BLK, terms), jnp.bfloat16),
        compiler_params=pltpu.CompilerParams(vmem_limit_bytes=32 << 20),
        name="fits",
    )(chosen, filled, *([res] * capacity), w)


def grouped(x, chans):
    tail = x.shape[2:]
    return jnp.swapaxes(x.reshape((2, chans // 8, 8) + tail), 0, 1)


def shards(stokes, lam2, peaks, island_owner, fit_matrix):
    freq = lax.axis_index("freq")
    freq_count, sky_count = lax.axis_size("freq"), lax.axis_size("sky")
    chans, local = lam2.shape[0], stokes.shape[1]
    rows, columns = stokes.shape[2], stokes.shape[3]
    capacity = max(2, 2 * island_owner.shape[0] // sky_count)
    weights = grouped(fit_matrix[0].reshape(2, chans, -1), chans).reshape(2 * chans, -1)
    weights = lax.all_gather(weights, "sky", axis=0)
    off, t = tables(lam2)
    pieces = stokes.reshape(2, local // 8, 8, rows, columns // BLK, BLK)
    send = jnp.transpose(pieces, (3, 4, 1, 0, 2, 5)).reshape(rows, columns // BLK, 2 * local, BLK)
    picks = lax.dynamic_index_in_dim(peaks, freq, 1, keepdims=False)
    picks = jnp.swapaxes(picks.reshape(-1, columns // BLK, BLK), 0, 1)
    res = clean_gather(send, picks, t, spread(off), chans)
    depths = DEPTHS // freq_count
    kt = synthesis(off, freq * depths, depths)
    chosen, filled = slots_of(island_owner[:, 0], sky_count, capacity)
    sent = fits(chosen, filled, res, weights)
    got = lax.all_to_all(sent, "sky", split_axis=0, concat_axis=0, tiled=True)
    return fdf(kt, res), got.astype(jnp.float32)[None]


def solution(mesh):
    in_specs = (
        P(None, "freq", "sky", None),
        P(),
        P(None, "sky", None),
        P("sky", None),
        P("sky", None, "freq"),
    )
    out_specs = (P(None, "freq", "sky", None), P("sky", None, None, None, "freq"))
    return jax.shard_map(shards, mesh=mesh, in_specs=in_specs, out_specs=out_specs, check_vma=False)
```

```python
import functools
import jax
import jax.numpy as jnp
from jax import lax
from jax.sharding import PartitionSpec as P
from jax.experimental import pallas as pl
from jax.experimental.pallas import tpu as pltpu

NC = 8
DEPTHS = 2048
STEP = 2.5
BLK = 128
LAG = 2
MESH = pl.DeviceIdType.MESH
GAIN = 0.3
LOW = 64

def gather(x, idx):
    return jnp.take_along_axis(x, idx, axis=1, mode="promise_in_bounds")


def full(row):
    return jnp.broadcast_to(row, (8, 128))


def make_tables(chans, column_ref, row_ref, t, near, spread):
    mean = jnp.sum(row_ref[...], axis=1, keepdims=True) / chans
    lane = lax.broadcasted_iota(jnp.int32, (8, 128), 1)
    low = lane < LOW
    depth = jnp.where(low, lane, (lane - LOW) * LOW - DEPTHS // 2).astype(jnp.float32) * STEP
    plain = lane.astype(jnp.float32) * STEP

    def rows(g, _):
        twice = 2.0 * (column_ref[pl.ds(pl.multiple_of(g * 8, 8), 8), :] - mean)
        angle = twice * depth
        parts = []
        for mask in (low, ~low):
            for value in (jnp.cos(angle), jnp.sin(angle)):
                value = jnp.where(mask, value, 0.0)
                top = value.astype(jnp.bfloat16)
                parts.append(jnp.concatenate([top, (value - top.astype(jnp.float32)).astype(jnp.bfloat16)], axis=1))
        t[pl.ds(pl.multiple_of(g * 32, 32), 32), :] = jnp.concatenate(parts, axis=0)
        angle = twice * plain
        near[0, pl.ds(pl.multiple_of(g * 8, 8), 8), :] = jnp.cos(angle)
        near[1, pl.ds(pl.multiple_of(g * 8, 8), 8), :] = jnp.sin(angle)
        return 0

    lax.fori_loop(0, chans // 8, rows, 0)
    twice = 2.0 * (row_ref[...] - mean)
    angle = twice * (lax.broadcasted_iota(jnp.int32, (16, chans), 0).astype(jnp.float32) * (128 * STEP))
    cosine, sine = jnp.cos(angle), jnp.sin(angle)
    dot = functools.partial(jnp.dot, precision=lax.Precision.HIGHEST, preferred_element_type=jnp.float32)
    spread[0] = (dot(cosine, near[0]) - dot(sine, near[1])) / chans
    spread[1] = -(dot(sine, near[0]) + dot(cosine, near[1])) / chans


def clean_tile(chans, row, rows, data, picks, t, spread, out_ref, oh, e4, ec, es):
    groups = chans // 8
    lo = picks & (LOW - 1)
    hi = (picks >> 6) + LOW
    index = lax.broadcasted_iota(jnp.int32, (128, 128), 0)
    for j in range(NC):
        cols = slice(j * 128, (j + 1) * 128)
        hot = ((index == lo[j:j+1]) | (index == hi[j:j+1])).astype(jnp.bfloat16)
        oh[0:128, cols] = hot
        oh[128:256, cols] = hot
    e4[...] = jnp.dot(t[...], oh[...], preferred_element_type=jnp.float32)

    def planes(g):
        at = pl.ds(g * (8 * rows) + row, 8, rows)
        return data[0, at, :], data[1, at, :]

    def peak(g, acc):
        q, u = planes(g)
        base = pl.multiple_of(g * 32, 32)
        out = []
        for j in range(NC):
            cols = slice(j * 128, (j + 1) * 128)
            cl, sl = e4[pl.ds(base, 8), cols], e4[pl.ds(base + 8, 8), cols]
            ch, sh = e4[pl.ds(base + 16, 8), cols], e4[pl.ds(base + 24, 8), cols]
            c = ch * cl - sh * sl
            s = sh * cl + ch * sl
            ec[g * NC + j] = c
            es[g * NC + j] = s
            out.append((acc[j][0] + (q * c + u * s), acc[j][1] + (u * c - q * s)))
        return tuple(out)

    zero = jnp.zeros((8, 128), jnp.float32)
    acc = lax.fori_loop(0, groups, peak, tuple((zero, zero) for _ in range(NC)))
    scale = 1.0 / chans
    vr = jnp.concatenate([jnp.sum(a[0], axis=0, keepdims=True) for a in acc], axis=0) * scale
    vi = jnp.concatenate([jnp.sum(a[1], axis=0, keepdims=True) for a in acc], axis=0) * scale
    comps = []
    for i in range(NC):
        cr = full(vr[i:i+1] * GAIN)
        ci = full(vi[i:i+1] * GAIN)
        comps.append((cr, ci))
        if i == NC - 1:
            break
        d = picks - picks[i:i+1]
        a = jnp.abs(d)
        alo, ahi = a & 127, a >> 7
        rr, ri = zero, zero
        for h in range(16):
            here = ahi == h
            rr = jnp.where(here, gather(full(spread[0, h:h+1, :]), alo), rr)
            ri = jnp.where(here, gather(full(spread[1, h:h+1, :]), alo), ri)
        ri = jnp.where(d < 0, -ri, ri)
        vr = vr - (cr * rr - ci * ri)
        vi = vi - (cr * ri + ci * rr)

    def model(pair, _):
        real, imag = [], []
        for part in range(2):
            g = pair * 2 + part
            q, u = planes(g)
            mr, mi = zero, zero
            for j in range(NC):
                c, s = ec[g * NC + j], es[g * NC + j]
                cr, ci = comps[j]
                mr = mr + (cr * c - ci * s)
                mi = mi + (cr * s + ci * c)
            real.append(q - mr)
            imag.append(u - mi)
        out_ref[pl.ds(pl.multiple_of(pair * 16, 16), 16), :] = jnp.concatenate(real, axis=0).astype(jnp.bfloat16)
        out_ref[pl.ds(pl.multiple_of(chans + pair * 16, 16), 16), :] = jnp.concatenate(imag, axis=0).astype(jnp.bfloat16)
        return 0

    lax.fori_loop(0, groups // 2, model, 0)


def island_kernel(chans, stokes_ref, column_ref, row_ref, picks_ref, owner_ref, w_ref, out_ref, sent_ref,
                  raw, data, res, w, fit, t, near, spread, oh, e4, ec, es, chosen,
                  own, sa, ra, sn, rn, sf, rf, so, ow, sw, rw, sc, rc):
    count = lax.axis_size("freq")
    me = lax.axis_index("freq")
    sky = lax.axis_index("sky")
    x, z, core = sky // 8, sky // 2 % 4, sky % 2
    chunks, rows = picks_ref.shape[0], stokes_ref.shape[2]
    tiles = chunks // rows
    local = stokes_ref.shape[1]
    half = chans
    left, right, far = [lax.rem(me + k, count) for k in (count - 1, 1, 2)]

    def at_x(k):
        return {"sky": lax.rem(x + k, 4) * 8 + z * 2 + core}

    def at_z(k):
        return {"sky": x * 8 + lax.rem(z + k, 4) * 2 + core}

    other = {"sky": sky + 1 - 2 * core}

    barrier = pltpu.get_barrier_semaphore()
    for k in range(1, 4):
        pl.semaphore_signal(barrier, inc=1, device_id={"freq": lax.rem(me + k, count)}, device_id_type=MESH)
        pl.semaphore_signal(barrier, inc=1, device_id=at_x(k), device_id_type=MESH)
        pl.semaphore_signal(barrier, inc=1, device_id=at_z(k), device_id_type=MESH)
    pl.semaphore_signal(barrier, inc=1, device_id=other, device_id_type=MESH)
    pl.semaphore_wait(barrier, 10)

    def columns(owner, tile):
        return pl.ds(pl.multiple_of((owner * tiles + tile) * 128, 128), 128)

    def part(tile, k):
        peer = lax.rem(me + k, count)
        return pltpu.make_async_remote_copy(
            src_ref=stokes_ref.at[:, :, :, columns(peer, tile)], dst_ref=raw.at[tile, me],
            send_sem=sa.at[tile, k], recv_sem=ra.at[tile, k], device_id={"freq": peer}, device_id_type=MESH)

    def arrived(tile, k):
        source = lax.rem(me + count - k, count)
        return pltpu.make_async_remote_copy(
            src_ref=stokes_ref.at[:, :, :, columns(me, tile)], dst_ref=raw.at[tile, source],
            send_sem=sa.at[tile, k], recv_sem=ra.at[tile, k], device_id={"freq": source}, device_id_type=MESH)

    def kept(tile):
        return pltpu.make_async_copy(stokes_ref.at[:, :, :, columns(me, tile)], raw.at[tile, me], own.at[tile])

    for tile in range(tiles):
        kept(tile).start()
        for k in (1, 3, 2):
            part(tile, k).start()
    pltpu.make_async_copy(w_ref.at[0], w.at[x, z, core], ow).start()
    pltpu.make_async_copy(w_ref.at[0], w.at[x, z, core], ow).wait()

    def w_first(h, k, source=None):
        along_x = h == 0
        lines = pl.ds(h * half, half)
        piece = w.at[x, z, core, lines]
        if source is not None:
            piece = w.at[lax.rem(x + 4 - k, 4), z, core, lines] if along_x else w.at[x, lax.rem(z + 4 - k, 4), core, lines]
        return pltpu.make_async_remote_copy(
            src_ref=piece, dst_ref=piece, send_sem=sw.at[0, h, k], recv_sem=rw.at[0, h, k],
            device_id=at_x(k) if along_x else at_z(k), device_id_type=MESH)

    def w_second(h, k, source=None):
        along_x = h == 1
        lines = pl.ds(h * half, half)
        back = k if source is not None else 4
        if along_x:
            piece = w.at[lax.rem(x + 4 - back + (4 if back == 4 else 0), 4), :, core, lines]
        else:
            piece = w.at[:, lax.rem(z + 4 - back + (4 if back == 4 else 0), 4), core, lines]
        return pltpu.make_async_remote_copy(
            src_ref=piece, dst_ref=piece, send_sem=sw.at[1, h, k], recv_sem=rw.at[1, h, k],
            device_id=at_x(k) if along_x else at_z(k), device_id_type=MESH)

    def w_third(which):
        piece = w.at[:, :, which]
        return pltpu.make_async_remote_copy(
            src_ref=piece, dst_ref=piece, send_sem=sc, recv_sem=rc, device_id=other, device_id_type=MESH)

    for h in range(2):
        for k in range(1, 4):
            w_first(h, k).start()

    def slot(o, _):
        first, second = jnp.int32(-1), jnp.int32(-1)
        for b in reversed(range(owner_ref.shape[0])):
            hit = owner_ref[b] == o
            second = jnp.where(hit, first, second)
            first = jnp.where(hit, b, first)
        chosen[o * 2] = first
        chosen[o * 2 + 1] = second
        return 0

    lax.fori_loop(0, sent_ref.shape[0], slot, 0)
    make_tables(chans, column_ref, row_ref, t, near, spread)

    def to_neighbour(c, way, source):
        return pltpu.make_async_remote_copy(
            src_ref=res.at[source, c], dst_ref=res.at[source, c],
            send_sem=sn.at[c, way], recv_sem=rn.at[c, way],
            device_id={"freq": right if way == 0 else left}, device_id_type=MESH)

    def onward(c, way, source):
        piece = res.at[source, c, pl.ds(way * half, half)]
        return pltpu.make_async_remote_copy(
            src_ref=piece, dst_ref=piece, send_sem=sf.at[c, way], recv_sem=rf.at[c, way],
            device_id={"freq": right if way == 0 else left}, device_id_type=MESH)

    def keep(c, source):
        return pltpu.make_async_copy(res.at[source, c], out_ref.at[source, c], so.at[c, source])

    def relay(c):
        to_neighbour(c, 0, left).wait_recv()
        onward(c, 0, left).start()
        keep(c, left).start()
        to_neighbour(c, 1, right).wait_recv()
        onward(c, 1, right).start()
        keep(c, right).start()

    def step(c, _):
        tile, row = c // rows, c % rows

        @pl.when(row == 0)
        def _():
            kept(tile).wait()
            for k in (1, 3, 2):
                arrived(tile, k).wait_recv()
            for source in range(count):
                for plane in range(2):
                    block = raw[tile, source, plane].reshape(local * rows, 128)
                    data[plane, source * local * rows:(source + 1) * local * rows, :] = block.astype(jnp.float32)

        clean_tile(chans, row, rows, data, picks_ref[c], t, spread, res.at[me, c], oh, e4, ec, es)
        to_neighbour(c, 0, me).start()
        to_neighbour(c, 1, me).start()
        keep(c, me).start()

        @pl.when(c >= LAG)
        def _():
            relay(c - LAG)

        @pl.when(c == 1)
        def _():
            for h in range(2):
                for k in range(1, 4):
                    w_first(h, k, True).wait_recv()
            for h in range(2):
                for k in range(1, 4):
                    w_second(h, k).start()

        @pl.when(c == 5)
        def _():
            for h in range(2):
                for k in range(1, 4):
                    w_second(h, k, True).wait_recv()
            w_third(core).start()

        return 0

    lax.fori_loop(0, chunks, step, 0)
    w_third(1 - core).wait_recv()

    def fit_block(source, c):
        b = c % rows * (count * tiles) + source * tiles + c // rows
        o = owner_ref[b]
        value = lax.dot_general(res[source, c], w[o >> 3, (o >> 1) & 3, o & 1], (((0,), (0,)), ((), ())),
                                preferred_element_type=jnp.float32)
        fit[b] = value.astype(jnp.bfloat16)

    def fit_some(sources, first, last):
        def some(c, _):
            for source in sources:
                fit_block(source, c)
            return 0
        lax.fori_loop(first, last, some, 0)

    fit_some((me,), 0, chunks)
    relay(chunks - 2)
    fit_some((left, right), 0, chunks // 2)
    relay(chunks - 1)
    fit_some((left, right), chunks // 2, chunks)

    def last(c, _):
        onward(c, 0, far).wait_recv()
        onward(c, 1, far).wait_recv()
        keep(c, far).start()
        fit_block(far, c)
        return 0

    lax.fori_loop(0, chunks, last, 0)

    def fill(o, _):
        for rank in range(2):
            b = chosen[o * 2 + rank]
            value = fit[jnp.maximum(b, 0)]
            sent_ref[o, rank] = jnp.where(b >= 0, value, jnp.zeros_like(value))
        return 0

    lax.fori_loop(0, sent_ref.shape[0], fill, 0)

    for tile in range(tiles):
        for k in (1, 3, 2):
            part(tile, k).wait_send()
    for h in range(2):
        for k in range(1, 4):
            w_first(h, k).wait_send()
            w_second(h, k).wait_send()
    w_third(core).wait_send()

    def finish(c, _):
        to_neighbour(c, 0, me).wait_send()
        to_neighbour(c, 1, me).wait_send()
        onward(c, 0, left).wait_send()
        onward(c, 1, right).wait_send()
        for source in (me, left, right, far):
            keep(c, source).wait()
        return 0

    lax.fori_loop(0, chunks, finish, 0)


def islands(stokes, lam2, picks, owners, weights, freq_count, sky_count):
    chans, local, rows = lam2.shape[0], stokes.shape[1], stokes.shape[2]
    groups = chans // 8
    chunks = picks.shape[0]
    terms = weights.shape[2]
    dma = pltpu.SemaphoreType.DMA
    vmem = pl.BlockSpec(memory_space=pltpu.VMEM)
    smem = pl.BlockSpec(memory_space=pltpu.SMEM)
    hbm = pl.BlockSpec(memory_space=pl.ANY)
    f32, bf16 = jnp.float32, jnp.bfloat16
    return pl.pallas_call(
        functools.partial(island_kernel, chans),
        in_specs=[hbm, vmem, vmem, vmem, smem, hbm],
        out_specs=[hbm, vmem],
        out_shape=[
            jax.ShapeDtypeStruct((freq_count, chunks, 2 * chans, 128), bf16),
            jax.ShapeDtypeStruct((sky_count, 2, BLK, terms), bf16),
        ],
        scratch_shapes=[
            pltpu.VMEM((chunks // rows, freq_count, 2, local, rows, 128), bf16),
            pltpu.VMEM((2, chans * rows, 128), f32),
            pltpu.VMEM((freq_count, chunks, 2 * chans, 128), bf16),
            pltpu.VMEM((4, 4, 2, 2 * chans, terms), bf16),
            pltpu.VMEM((freq_count * chunks, BLK, terms), bf16),
            pltpu.VMEM((4 * chans, 256), bf16),
            pltpu.VMEM((2, chans, 128), f32),
            pltpu.VMEM((2, 16, 128), f32),
            pltpu.VMEM((256, NC * 128), bf16),
            pltpu.VMEM((4 * chans, NC * 128), f32),
            pltpu.VMEM((groups * NC, 8, 128), f32),
            pltpu.VMEM((groups * NC, 8, 128), f32),
            pltpu.SMEM((sky_count * 2,), jnp.int32),
            dma((chunks // rows,)), dma((chunks // rows, 4)), dma((chunks // rows, 4)),
            dma((chunks, 2)), dma((chunks, 2)), dma((chunks, 2)), dma((chunks, 2)), dma((chunks, 4)),
            dma, dma((2, 2, 4)), dma((2, 2, 4)), dma, dma,
        ],
        compiler_params=pltpu.CompilerParams(collective_id=0, has_side_effects=True, vmem_limit_bytes=50 << 20),
        cost_estimate=pl.CostEstimate(flops=3 << 32, bytes_accessed=16 << 20, transcendentals=0),
        name="islands",
    )(stokes, lam2.reshape(chans, 1), lam2.reshape(1, chans), picks, owners, weights)


def synthesis(lam2, first, count):
    chans = lam2.shape[0]
    off = lam2 - jnp.mean(lam2)
    depth = (jnp.arange(count) + first - DEPTHS // 2).astype(jnp.float32) * STEP
    angle = (2.0 * off) * depth[:, None]
    cosine, sine = jnp.cos(angle), jnp.sin(angle)
    real = jnp.concatenate([cosine, sine], axis=1)
    imag = jnp.concatenate([-sine, cosine], axis=1)
    return (jnp.concatenate([real, imag], axis=0) / chans).astype(jnp.bfloat16)


def fdf_kernel(k_ref, res_ref, out_ref, mixed):
    rows, depths = res_ref.shape[2], k_ref.shape[0]
    for pair in range(0, rows, 2):
        block = jnp.concatenate([res_ref[0, 0, pair], res_ref[0, 0, pair + 1]], axis=1)
        for first in range(0, depths, 256):
            part = jnp.dot(k_ref[first:first + 256, :], block, preferred_element_type=jnp.float32)
            for row in range(2):
                mixed[pl.ds(first * rows + pair + row, 256, rows), :] = part[:, row * 128:(row + 1) * 128]
    out_ref[...] = mixed[...].astype(jnp.bfloat16).reshape(out_ref.shape)


def fdf(kt, res, rows):
    count, chunks, total, _ = res.shape
    tiles = chunks // rows
    depths = kt.shape[0]
    columns = count * tiles * 128
    return pl.pallas_call(
        fdf_kernel,
        grid=(count * tiles,),
        in_specs=[
            pl.BlockSpec((depths, total), lambda i: (0, 0)),
            pl.BlockSpec((1, 1, rows, total, 128), lambda i: (i // tiles, i % tiles, 0, 0, 0)),
        ],
        out_specs=pl.BlockSpec((2, depths // 2, rows, 128), lambda i: (0, 0, 0, i)),
        out_shape=jax.ShapeDtypeStruct((2, depths // 2, rows, columns), jnp.bfloat16),
        scratch_shapes=[pltpu.VMEM((depths * rows, 128), jnp.float32)],
        compiler_params=pltpu.CompilerParams(vmem_limit_bytes=48 << 20),
        cost_estimate=pl.CostEstimate(flops=2 * depths * total * rows * columns, bytes_accessed=14 << 20, transcendentals=0),
        name="fdf",
    )(kt, res.reshape(count, tiles, rows, total, 128))


def shards(stokes, lam2, peaks, island_owner, fit_matrix):
    freq = lax.axis_index("freq")
    freq_count, sky_count = lax.axis_size("freq"), lax.axis_size("sky")
    rows, columns = stokes.shape[2], stokes.shape[3]
    mine = columns // freq_count
    picks = lax.dynamic_slice_in_dim(peaks, freq * mine, mine, 2)
    picks = jnp.transpose(picks.reshape(NC, rows, mine // 128, 128), (2, 1, 0, 3)).reshape(-1, NC, 128)
    res, sent = islands(stokes, lam2, picks, island_owner[:, 0], fit_matrix, freq_count, sky_count)
    depths = DEPTHS // freq_count
    kt = synthesis(lam2, freq * depths, depths)
    got = lax.all_to_all(sent, "sky", split_axis=0, concat_axis=0, tiled=True)
    return fdf(kt, res, rows), got.astype(jnp.float32)[None]


def solution(mesh):
    in_specs = (
        P(None, "freq", "sky", None),
        P(),
        P(None, "sky", None),
        P("sky", None),
        P("sky", None, "freq"),
    )
    out_specs = (P(None, "freq", "sky", None), P("sky", None, None, None, "freq"))
    return jax.shard_map(shards, mesh=mesh, in_specs=in_specs, out_specs=out_specs, check_vma=False)
```

```python
import functools
import jax
import jax.numpy as jnp
from jax import lax
from jax.sharding import PartitionSpec as P
from jax.experimental import pallas as pl
from jax.experimental.pallas import tpu as pltpu

NC = 8
DEPTHS = 2048
STEP = 2.5
BLK = 128
LAG = 2
MESH = pl.DeviceIdType.MESH
GAIN = 0.3
LOW = 64

def gather(x, idx):
    return jnp.take_along_axis(x, idx, axis=1, mode="promise_in_bounds")


def full(row):
    return jnp.broadcast_to(row, (8, 128))


def make_tables(chans, column_ref, row_ref, t, near, spread):
    mean = jnp.sum(row_ref[...], axis=1, keepdims=True) / (2 * chans)
    lane = lax.broadcasted_iota(jnp.int32, (8, 128), 1)
    low = lane < LOW
    depth = jnp.where(low, lane, (lane - LOW) * LOW - DEPTHS // 2).astype(jnp.float32) * STEP
    plain = lane.astype(jnp.float32) * STEP

    def rows(g, _):
        twice = 2.0 * (column_ref[pl.ds(pl.multiple_of(g * 8, 8), 8), :] - mean)
        angle = twice * depth
        parts = []
        for mask in (low, ~low):
            for value in (jnp.cos(angle), jnp.sin(angle)):
                value = jnp.where(mask, value, 0.0)
                top = value.astype(jnp.bfloat16)
                parts.append(jnp.concatenate([top, (value - top.astype(jnp.float32)).astype(jnp.bfloat16)], axis=1))
        t[pl.ds(pl.multiple_of(g * 32, 32), 32), :] = jnp.concatenate(parts, axis=0)
        angle = twice * plain
        near[0, pl.ds(pl.multiple_of(g * 8, 8), 8), :] = jnp.cos(angle)
        near[1, pl.ds(pl.multiple_of(g * 8, 8), 8), :] = jnp.sin(angle)
        return 0

    lax.fori_loop(0, chans // 8, rows, 0)
    twice = 2.0 * (row_ref[:, :chans] - mean)
    angle = twice * (lax.broadcasted_iota(jnp.int32, (16, chans), 0).astype(jnp.float32) * (128 * STEP))
    cosine, sine = jnp.cos(angle), jnp.sin(angle)
    dot = functools.partial(jnp.dot, precision=lax.Precision.HIGHEST, preferred_element_type=jnp.float32)
    spread[0] = (dot(cosine, near[0]) - dot(sine, near[1])) / chans
    spread[1] = -(dot(sine, near[0]) + dot(cosine, near[1])) / chans


def make_synthesis(chans, row_ref, first, kt, ck, sk):
    total = 2 * chans
    depths = kt.shape[0] // 2
    mean = jnp.sum(row_ref[...], axis=1, keepdims=True) / total
    twice = 2.0 * (row_ref[...] - mean)
    fine = twice * (lax.broadcasted_iota(jnp.int32, (LOW, total), 0).astype(jnp.float32) * STEP)
    ck[...] = jnp.cos(fine)
    sk[...] = jnp.sin(fine)
    steps = lax.broadcasted_iota(jnp.int32, (8, total), 0) * LOW + (first - DEPTHS // 2)
    coarse = twice * (steps.astype(jnp.float32) * STEP)
    cosine, sine = jnp.cos(coarse), jnp.sin(coarse)
    is_q = lax.broadcasted_iota(jnp.int32, (16, total), 1) < chans
    for h in range(depths // LOW):
        ch, sh = cosine[h:h+1], sine[h:h+1]
        for l in range(0, LOW, 16):
            cl, sl = ck[l:l+16, :], sk[l:l+16, :]
            c = (ch * cl - sh * sl) / chans
            s = (sh * cl + ch * sl) / chans
            at = h * LOW + l
            kt[at:at+16, :] = jnp.where(is_q, c, s).astype(jnp.bfloat16)
            kt[depths+at:depths+at+16, :] = jnp.where(is_q, -s, c).astype(jnp.bfloat16)


def synthesize(source, tile, tiles, kt, res, mixed, stage):
    rows, depths = 2 * tiles, kt.shape[0]
    for pair in range(2):
        a = res[source, tile * 2 + pair]
        b = res[source, tiles * 2 + tile * 2 + pair]
        block = jnp.concatenate([a[:, :64], b[:, :64], a[:, 64:], b[:, 64:]], axis=1)
        for first in range(0, depths, 256):
            part = jnp.dot(kt[first:first + 256, :], block, preferred_element_type=jnp.float32)
            for row in range(2):
                mixed[pl.ds(first * rows + pair * 2 + row, 256, rows), :] = part[:, row * 128:(row + 1) * 128]
    stage[...] = mixed[...].astype(jnp.bfloat16).reshape(stage.shape)


def clean_tile(chans, pair, half, rows, data, peaks, t, spread, out_ref, oh, e4, ec, es, joint):
    groups = chans // 8
    stays, moves = pair * 2 + half, pair * 2 + 1 - half
    here = (lax.broadcasted_iota(jnp.int32, (8, 128), 1) < 64) == (half == 0)

    def merged(ref, base):
        kept = ref[pl.ds(base + stays, 8, rows), :]
        moved = ref[pl.ds(base + moves, 8, rows), :]
        return jnp.where(here, kept, pltpu.roll(moved, 64, 1))

    picks = merged(peaks, 0)
    lo = picks & (LOW - 1)
    hi = (picks >> 6) + LOW
    index = lax.broadcasted_iota(jnp.int32, (128, 128), 0)
    for j in range(NC):
        cols = slice(j * 128, (j + 1) * 128)
        hot = ((index == lo[j:j+1]) | (index == hi[j:j+1])).astype(jnp.bfloat16)
        oh[0:128, cols] = hot
        oh[128:256, cols] = hot
    e4[...] = jnp.dot(t[...], oh[...], preferred_element_type=jnp.float32)

    def peak(g, acc):
        q, u = merged(data.at[0], g * (8 * rows)), merged(data.at[1], g * (8 * rows))
        joint[0, g] = q
        joint[1, g] = u
        base = pl.multiple_of(g * 32, 32)
        out = []
        for j in range(NC):
            cols = slice(j * 128, (j + 1) * 128)
            cl, sl = e4[pl.ds(base, 8), cols], e4[pl.ds(base + 8, 8), cols]
            ch, sh = e4[pl.ds(base + 16, 8), cols], e4[pl.ds(base + 24, 8), cols]
            c = ch * cl - sh * sl
            s = sh * cl + ch * sl
            ec[g * NC + j] = c
            es[g * NC + j] = s
            out.append((acc[j][0] + (q * c + u * s), acc[j][1] + (u * c - q * s)))
        return tuple(out)

    zero = jnp.zeros((8, 128), jnp.float32)
    acc = lax.fori_loop(0, groups, peak, tuple((zero, zero) for _ in range(NC)))
    scale = 1.0 / chans
    vr = jnp.concatenate([jnp.sum(a[0], axis=0, keepdims=True) for a in acc], axis=0) * scale
    vi = jnp.concatenate([jnp.sum(a[1], axis=0, keepdims=True) for a in acc], axis=0) * scale
    comps = []
    for i in range(NC):
        cr = full(vr[i:i+1] * GAIN)
        ci = full(vi[i:i+1] * GAIN)
        comps.append((cr, ci))
        if i == NC - 1:
            break
        d = picks - picks[i:i+1]
        a = jnp.abs(d)
        alo, ahi = a & 127, a >> 7
        rr, ri = zero, zero
        for h in range(16):
            here = ahi == h
            rr = jnp.where(here, gather(full(spread[0, h:h+1, :]), alo), rr)
            ri = jnp.where(here, gather(full(spread[1, h:h+1, :]), alo), ri)
        ri = jnp.where(d < 0, -ri, ri)
        vr = vr - (cr * rr - ci * ri)
        vi = vi - (cr * ri + ci * rr)

    def model(pair, _):
        real, imag = [], []
        for part in range(2):
            g = pair * 2 + part
            q, u = joint[0, g], joint[1, g]
            mr, mi = zero, zero
            for j in range(NC):
                c, s = ec[g * NC + j], es[g * NC + j]
                cr, ci = comps[j]
                mr = mr + (cr * c - ci * s)
                mi = mi + (cr * s + ci * c)
            real.append(q - mr)
            imag.append(u - mi)
        out_ref[pl.ds(pl.multiple_of(pair * 16, 16), 16), :] = jnp.concatenate(real, axis=0).astype(jnp.bfloat16)
        out_ref[pl.ds(pl.multiple_of(chans + pair * 16, 16), 16), :] = jnp.concatenate(imag, axis=0).astype(jnp.bfloat16)
        return 0

    lax.fori_loop(0, groups // 2, model, 0)


def island_kernel(chans, stokes_ref, column_ref, row_ref, peaks_ref, owner_ref, w_ref, out_ref, got_ref,
                  raw, data, res, w, fit, sent, t, near, spread, kt, ck, sk, peaks, joint_peaks, mixed, stage, oh, e4, ec, es, joint, chosen,
                  own, sa, ra, sn, rn, sf, rf, so, ow, op, sw, rw, sc, rc, sd, rd, od):
    count, skies = lax.axis_size("freq"), lax.axis_size("sky")
    me = lax.axis_index("freq")
    sky = lax.axis_index("sky")
    x, z, core = sky // 8, sky // 2 % 4, sky % 2
    rows = stokes_ref.shape[2]
    tiles = stokes_ref.shape[3] // (count * 128)
    chunks = rows * tiles
    halfway = chunks // 2
    local = stokes_ref.shape[1]
    half = chans
    left, right, far = [lax.rem(me + k, count) for k in (count - 1, 1, 2)]

    def at_x(k):
        return {"sky": lax.rem(x + k, 4) * 8 + z * 2 + core}

    def at_z(k):
        return {"sky": x * 8 + lax.rem(z + k, 4) * 2 + core}

    other = {"sky": sky + 1 - 2 * core}

    barrier = pltpu.get_barrier_semaphore()
    for k in range(1, 4):
        pl.semaphore_signal(barrier, inc=1, device_id={"freq": lax.rem(me + k, count)}, device_id_type=MESH)

    def greet(k, _):
        pl.semaphore_signal(barrier, inc=1, device_id={"sky": lax.rem(sky + k, skies)}, device_id_type=MESH)
        return 0

    lax.fori_loop(1, skies, greet, 0)
    pl.semaphore_wait(barrier, count + skies - 2)

    def columns(owner, tile):
        return pl.ds(pl.multiple_of((owner * tiles + tile) * 128, 128), 128)

    def part(tile, k):
        peer = lax.rem(me + k, count)
        return pltpu.make_async_remote_copy(
            src_ref=stokes_ref.at[:, :, :, columns(peer, tile)], dst_ref=raw.at[tile, me],
            send_sem=sa.at[tile, k], recv_sem=ra.at[tile, k], device_id={"freq": peer}, device_id_type=MESH)

    def arrived(tile, k):
        source = lax.rem(me + count - k, count)
        return pltpu.make_async_remote_copy(
            src_ref=stokes_ref.at[:, :, :, columns(me, tile)], dst_ref=raw.at[tile, source],
            send_sem=sa.at[tile, k], recv_sem=ra.at[tile, k], device_id={"freq": source}, device_id_type=MESH)

    def kept(tile):
        return pltpu.make_async_copy(stokes_ref.at[:, :, :, columns(me, tile)], raw.at[tile, me], own.at[tile])

    for tile in range(tiles):
        kept(tile).start()
        for k in (1, 3, 2):
            part(tile, k).start()
    mine = pl.ds(pl.multiple_of(me * (tiles * 128), 128), tiles * 128)
    pltpu.make_async_copy(peaks_ref.at[:, :, mine], peaks, op).start()
    pltpu.make_async_copy(w_ref.at[0], w.at[x, z, core], ow).start()
    pltpu.make_async_copy(w_ref.at[0], w.at[x, z, core], ow).wait()

    def w_first(h, k, source=None):
        along_x = h == 0
        lines = pl.ds(h * half, half)
        piece = w.at[x, z, core, lines]
        if source is not None:
            piece = w.at[lax.rem(x + 4 - k, 4), z, core, lines] if along_x else w.at[x, lax.rem(z + 4 - k, 4), core, lines]
        return pltpu.make_async_remote_copy(
            src_ref=piece, dst_ref=piece, send_sem=sw.at[0, h, k], recv_sem=rw.at[0, h, k],
            device_id=at_x(k) if along_x else at_z(k), device_id_type=MESH)

    def w_second(h, k, source=None):
        along_x = h == 1
        lines = pl.ds(h * half, half)
        back = k if source is not None else 4
        if along_x:
            piece = w.at[lax.rem(x + 4 - back + (4 if back == 4 else 0), 4), :, core, lines]
        else:
            piece = w.at[:, lax.rem(z + 4 - back + (4 if back == 4 else 0), 4), core, lines]
        return pltpu.make_async_remote_copy(
            src_ref=piece, dst_ref=piece, send_sem=sw.at[1, h, k], recv_sem=rw.at[1, h, k],
            device_id=at_x(k) if along_x else at_z(k), device_id_type=MESH)

    def w_third(which):
        piece = w.at[:, :, which]
        return pltpu.make_async_remote_copy(
            src_ref=piece, dst_ref=piece, send_sem=sc, recv_sem=rc, device_id=other, device_id_type=MESH)

    for h in range(2):
        for k in range(1, 4):
            w_first(h, k).start()

    def slot(o, _):
        first, second = jnp.int32(-1), jnp.int32(-1)
        for b in reversed(range(owner_ref.shape[0])):
            hit = owner_ref[b] == o
            second = jnp.where(hit, first, second)
            first = jnp.where(hit, b, first)
        chosen[o * 2] = first
        chosen[o * 2 + 1] = second
        return 0

    lax.fori_loop(0, skies, slot, 0)
    make_tables(chans, column_ref, row_ref, t, near, spread)

    def to_neighbour(c, way, source):
        return pltpu.make_async_remote_copy(
            src_ref=res.at[source, c], dst_ref=res.at[source, c],
            send_sem=sn.at[c, way], recv_sem=rn.at[c, way],
            device_id={"freq": right if way == 0 else left}, device_id_type=MESH)

    def onward(c, way, source):
        piece = res.at[source, c, pl.ds(way * half, half)]
        return pltpu.make_async_remote_copy(
            src_ref=piece, dst_ref=piece, send_sem=sf.at[c, way], recv_sem=rf.at[c, way],
            device_id={"freq": right if way == 0 else left}, device_id_type=MESH)

    def relay(c):
        to_neighbour(c, 0, left).wait_recv()
        onward(c, 0, left).start()
        to_neighbour(c, 1, right).wait_recv()
        onward(c, 1, right).start()

    def fit_chunk(source, c):
        part, tile, pair = c // halfway, c // 2 % tiles, c % 2
        b = pair * (2 * count * tiles) + source * tiles + tile
        after = b + count * tiles
        o, p = owner_ref[b], owner_ref[after]
        both = jnp.concatenate([w[o >> 3, (o >> 1) & 3, o & 1], w[p >> 3, (p >> 1) & 3, p & 1]], axis=1)
        value = lax.dot_general(res[source, c], both, (((0,), (0,)), ((), ())), preferred_element_type=jnp.float32)
        terms = value.shape[1] // 2
        fit[part, b] = value[:64, :terms].astype(jnp.bfloat16)
        fit[part, after] = value[64:, terms:].astype(jnp.bfloat16)

    def fit_some(sources, first, last):
        def some(c, _):
            for source in sources:
                fit_chunk(source, c)
            return 0
        lax.fori_loop(first, last, some, 0)

    def fit_far(first, last):
        def some(c, _):
            onward(c, 0, far).wait_recv()
            onward(c, 1, far).wait_recv()
            fit_chunk(far, c)
            return 0
        lax.fori_loop(first, last, some, 0)

    def result(part, k, source):
        peer = lax.rem(sky + k, skies)
        return pltpu.make_async_remote_copy(
            src_ref=sent.at[part, peer], dst_ref=got_ref.at[source, :, pl.ds(part * 64, 64)],
            send_sem=sd.at[part, k], recv_sem=rd.at[part, k], device_id={"sky": peer}, device_id_type=MESH)

    def kept_result(part):
        return pltpu.make_async_copy(sent.at[part, sky], got_ref.at[sky, :, pl.ds(part * 64, 64)], od.at[part])

    def send_results(part):
        def fill(o, _):
            for rank in range(2):
                b = chosen[o * 2 + rank]
                value = fit[part, jnp.maximum(b, 0)]
                sent[part, o, rank] = jnp.where(b >= 0, value, jnp.zeros_like(value))
            return 0

        def send(k, _):
            result(part, k, sky).start()
            return 0

        lax.fori_loop(0, skies, fill, 0)
        lax.fori_loop(1, skies, send, 0)
        kept_result(part).start()

    pltpu.make_async_copy(peaks_ref.at[:, :, mine], peaks, op).wait()

    def step(c, _):
        part, tile, pair = c // halfway, c // 2 % tiles, c % 2

        @pl.when((pair == 0) & (part == 0))
        def _():
            kept(tile).wait()
            for k in (1, 3, 2):
                arrived(tile, k).wait_recv()
            for source in range(count):
                for plane in range(2):
                    block = raw[tile, source, plane].reshape(local * rows, 128)
                    data[tile, plane, source * local * rows:(source + 1) * local * rows, :] = block.astype(jnp.float32)
            joint_peaks[tile] = peaks[:, :, pl.ds(pl.multiple_of(tile * 128, 128), 128)].reshape(NC * rows, 128)

        clean_tile(chans, pair, part, rows, data.at[tile], joint_peaks.at[tile], t, spread, res.at[me, c], oh, e4, ec, es, joint)
        to_neighbour(c, 0, me).start()
        to_neighbour(c, 1, me).start()

        @pl.when(c >= LAG)
        def _():
            relay(c - LAG)

        @pl.when(c == 1)
        def _():
            for h in range(2):
                for k in range(1, 4):
                    w_first(h, k, True).wait_recv()
            for h in range(2):
                for k in range(1, 4):
                    w_second(h, k).start()
            make_synthesis(chans, row_ref, me * (kt.shape[0] // 2), kt, ck, sk)

        @pl.when(c == 4)
        def _():
            for h in range(2):
                for k in range(1, 4):
                    w_second(h, k, True).wait_recv()
            w_third(core).start()

        @pl.when(c == 5)
        def _():
            w_third(1 - core).wait_recv()
            fit_some((me,), 0, halfway)
            fit_some((left, right), 0, halfway - 1)

        @pl.when(c == 6)
        def _():
            fit_some((left, right), halfway - 1, halfway)
            fit_far(0, halfway)
            send_results(0)

        return 0

    lax.fori_loop(0, chunks, step, 0)
    fit_some((me,), halfway, chunks)
    relay(chunks - 2)
    fit_some((left, right), halfway, chunks - 1)
    relay(chunks - 1)
    fit_far(halfway, chunks - 1)
    fit_some((left, right), chunks - 1, chunks)
    fit_far(chunks - 1, chunks)
    send_results(1)

    def put(u):
        cols = pl.ds(pl.multiple_of(u * 128, 128), 128)
        return pltpu.make_async_copy(stage.at[u % 2], out_ref.at[:, :, :, cols], so.at[u])

    def unit(u, _):
        @pl.when(u >= 2)
        def _():
            put(u - 2).wait()

        synthesize(u // tiles, u % tiles, tiles, kt, res, mixed, stage.at[u % 2])
        put(u).start()
        return 0

    lax.fori_loop(0, count * tiles, unit, 0)
    put(count * tiles - 2).wait()
    put(count * tiles - 1).wait()

    for tile in range(tiles):
        for k in (1, 3, 2):
            part(tile, k).wait_send()
    for h in range(2):
        for k in range(1, 4):
            w_first(h, k).wait_send()
            w_second(h, k).wait_send()
    w_third(core).wait_send()

    def finish(c, _):
        to_neighbour(c, 0, me).wait_send()
        to_neighbour(c, 1, me).wait_send()
        onward(c, 0, left).wait_send()
        onward(c, 1, right).wait_send()
        return 0

    lax.fori_loop(0, chunks, finish, 0)
    for which in range(2):
        kept_result(which).wait()

        def results(k, _):
            result(which, k, lax.rem(sky + skies - k, skies)).wait_recv()
            result(which, k, sky).wait_send()
            return 0

        lax.fori_loop(1, skies, results, 0)


def islands(stokes, lam2, peaks, owners, weights, freq_count, sky_count):
    chans, local, rows, columns = lam2.shape[0], stokes.shape[1], stokes.shape[2], stokes.shape[3]
    groups = chans // 8
    tiles = columns // (freq_count * 128)
    chunks = rows * tiles
    terms = weights.shape[2]
    depths = DEPTHS // freq_count
    dma = pltpu.SemaphoreType.DMA
    vmem = pl.BlockSpec(memory_space=pltpu.VMEM)
    smem = pl.BlockSpec(memory_space=pltpu.SMEM)
    hbm = pl.BlockSpec(memory_space=pl.ANY)
    f32, bf16 = jnp.float32, jnp.bfloat16
    return pl.pallas_call(
        functools.partial(island_kernel, chans),
        in_specs=[hbm, vmem, vmem, hbm, smem, hbm],
        out_specs=[hbm, hbm],
        out_shape=[
            jax.ShapeDtypeStruct((2, depths, rows, columns), bf16),
            jax.ShapeDtypeStruct((sky_count, 2, BLK, terms), bf16),
        ],
        scratch_shapes=[
            pltpu.VMEM((tiles, freq_count, 2, local, rows, 128), bf16),
            pltpu.VMEM((tiles, 2, chans * rows, 128), f32),
            pltpu.VMEM((freq_count, chunks, 2 * chans, 128), bf16),
            pltpu.VMEM((4, 4, 2, 2 * chans, terms), bf16),
            pltpu.VMEM((2, freq_count * chunks, 64, terms), bf16),
            pltpu.VMEM((2, sky_count, 2, 64, terms), bf16),
            pltpu.VMEM((4 * chans, 256), bf16),
            pltpu.VMEM((2, chans, 128), f32),
            pltpu.VMEM((2, 16, 128), f32),
            pltpu.VMEM((2 * depths, 2 * chans), bf16),
            pltpu.VMEM((LOW, 2 * chans), f32),
            pltpu.VMEM((LOW, 2 * chans), f32),
            pltpu.VMEM((NC, rows, tiles * 128), jnp.int32),
            pltpu.VMEM((tiles, NC * rows, 128), jnp.int32),
            pltpu.VMEM((2 * depths * rows, 128), f32),
            pltpu.VMEM((2, 2, depths, rows, 128), bf16),
            pltpu.VMEM((256, NC * 128), bf16),
            pltpu.VMEM((4 * chans, NC * 128), f32),
            pltpu.VMEM((groups * NC, 8, 128), f32),
            pltpu.VMEM((groups * NC, 8, 128), f32),
            pltpu.VMEM((2, groups, 8, 128), f32),
            pltpu.SMEM((sky_count * 2,), jnp.int32),
            dma((tiles,)), dma((tiles, 4)), dma((tiles, 4)),
            dma((chunks, 2)), dma((chunks, 2)), dma((chunks, 2)), dma((chunks, 2)), dma((freq_count * tiles,)),
            dma, dma, dma((2, 2, 4)), dma((2, 2, 4)), dma, dma,
            dma((2, sky_count)), dma((2, sky_count)), dma((2,)),
        ],
        compiler_params=pltpu.CompilerParams(collective_id=0, has_side_effects=True, vmem_limit_bytes=60 << 20),
        cost_estimate=pl.CostEstimate(flops=6 << 32, bytes_accessed=24 << 20, transcendentals=0),
        name="islands",
    )(stokes, lam2.reshape(chans, 1), jnp.concatenate([lam2, lam2]).reshape(1, 2 * chans), peaks, owners, weights)


def shards(stokes, lam2, peaks, island_owner, fit_matrix):
    freq_count, sky_count = lax.axis_size("freq"), lax.axis_size("sky")
    residual_fdf, got = islands(stokes, lam2, peaks, island_owner[:, 0], fit_matrix, freq_count, sky_count)
    return residual_fdf, got.astype(jnp.float32)[None]


def solution(mesh):
    in_specs = (
        P(None, "freq", "sky", None),
        P(),
        P(None, "sky", None),
        P("sky", None),
        P("sky", None, "freq"),
    )
    out_specs = (P(None, "freq", "sky", None), P("sky", None, None, None, "freq"))
    return jax.shard_map(shards, mesh=mesh, in_specs=in_specs, out_specs=out_specs, check_vma=False)
```

```python
import functools
import jax
import jax.numpy as jnp
from jax import lax
from jax.sharding import PartitionSpec as P
from jax.experimental import pallas as pl
from jax.experimental.pallas import tpu as pltpu

NC = 8
DEPTHS = 2048
STEP = 2.5
BLK = 128
LAG = 2
MESH = pl.DeviceIdType.MESH
GAIN = 0.3
LOW = 64

def gather(x, idx):
    return jnp.take_along_axis(x, idx, axis=1, mode="promise_in_bounds")


def full(row):
    return jnp.broadcast_to(row, (8, 128))


def make_tables(chans, row_ref, t, near, spread):
    mean = jnp.sum(row_ref[...], axis=1, keepdims=True) / chans
    along = jnp.broadcast_to(row_ref[...] - mean, (8, chans))
    place = lax.broadcasted_iota(jnp.int32, (8, chans), 1) - lax.broadcasted_iota(jnp.int32, (8, chans), 0)
    lane = lax.broadcasted_iota(jnp.int32, (8, 128), 1)
    low = lane < LOW
    depth = jnp.where(low, lane, (lane - LOW) * LOW - DEPTHS // 2).astype(jnp.float32) * STEP
    plain = lane.astype(jnp.float32) * STEP

    def rows(g, _):
        twice = 2.0 * jnp.sum(jnp.where(place == g * 8, along, 0.0), axis=1, keepdims=True)
        angle = twice * depth
        parts = []
        for mask in (low, ~low):
            for value in (jnp.cos(angle), jnp.sin(angle)):
                value = jnp.where(mask, value, 0.0)
                top = value.astype(jnp.bfloat16)
                parts.append(jnp.concatenate([top, (value - top.astype(jnp.float32)).astype(jnp.bfloat16)], axis=1))
        t[pl.ds(pl.multiple_of(g * 32, 32), 32), :] = jnp.concatenate(parts, axis=0)
        angle = twice * plain
        near[0, pl.ds(pl.multiple_of(g * 8, 8), 8), :] = jnp.cos(angle)
        near[1, pl.ds(pl.multiple_of(g * 8, 8), 8), :] = jnp.sin(angle)
        return 0

    lax.fori_loop(0, chans // 8, rows, 0)
    twice = 2.0 * (row_ref[...] - mean)
    angle = twice * (lax.broadcasted_iota(jnp.int32, (16, chans), 0).astype(jnp.float32) * (128 * STEP))
    cosine, sine = jnp.cos(angle), jnp.sin(angle)
    dot = functools.partial(jnp.dot, precision=lax.Precision.HIGHEST, preferred_element_type=jnp.float32)
    spread[0] = (dot(cosine, near[0]) - dot(sine, near[1])) / chans
    spread[1] = -(dot(sine, near[0]) + dot(cosine, near[1])) / chans


def make_synthesis(chans, row_ref, first, kt, ck, sk):
    total = 2 * chans
    depths = kt.shape[0] // 2
    mean = jnp.sum(row_ref[...], axis=1, keepdims=True) / chans
    twice = 2.0 * (row_ref[...] - mean)
    twice = jnp.concatenate([twice, twice], axis=1)
    fine = twice * (lax.broadcasted_iota(jnp.int32, (LOW, total), 0).astype(jnp.float32) * STEP)
    ck[...] = jnp.cos(fine)
    sk[...] = jnp.sin(fine)
    steps = lax.broadcasted_iota(jnp.int32, (8, total), 0) * LOW + (first - DEPTHS // 2)
    coarse = twice * (steps.astype(jnp.float32) * STEP)
    cosine, sine = jnp.cos(coarse), jnp.sin(coarse)
    is_q = lax.broadcasted_iota(jnp.int32, (16, total), 1) < chans
    for h in range(depths // LOW):
        ch, sh = cosine[h:h+1], sine[h:h+1]
        for l in range(0, LOW, 16):
            cl, sl = ck[l:l+16, :], sk[l:l+16, :]
            c = (ch * cl - sh * sl) / chans
            s = (sh * cl + ch * sl) / chans
            at = h * LOW + l
            kt[at:at+16, :] = jnp.where(is_q, c, s).astype(jnp.bfloat16)
            kt[depths+at:depths+at+16, :] = jnp.where(is_q, -s, c).astype(jnp.bfloat16)


def fdf_kernel(k_ref, res_ref, out_ref, mixed):
    rows, depths = out_ref.shape[2], k_ref.shape[0]
    for pair in range(rows // 2):
        a, b = res_ref[0, 0, 0, pair], res_ref[0, 1, 0, pair]
        block = jnp.concatenate([a[:, :64], b[:, :64], a[:, 64:], b[:, 64:]], axis=1)
        for first in range(0, depths, 256):
            part = jnp.dot(k_ref[first:first + 256, :], block, preferred_element_type=jnp.float32)
            for row in range(2):
                mixed[pl.ds(first * rows + pair * 2 + row, 256, rows), :] = part[:, row * 128:(row + 1) * 128]
    out_ref[...] = mixed[...].astype(jnp.bfloat16).reshape(out_ref.shape)


def fdf(kt, res, rows):
    count, chunks, total, _ = res.shape
    tiles = chunks // rows
    depths = kt.shape[0]
    columns = count * tiles * 128
    return pl.pallas_call(
        fdf_kernel,
        grid=(count * tiles,),
        in_specs=[
            pl.BlockSpec((depths, total), lambda i: (0, 0)),
            pl.BlockSpec((1, 2, 1, rows // 2, total, 128), lambda i: (i // tiles, 0, i % tiles, 0, 0, 0)),
        ],
        out_specs=pl.BlockSpec((2, depths // 2, rows, 128), lambda i: (0, 0, 0, i)),
        out_shape=jax.ShapeDtypeStruct((2, depths // 2, rows, columns), jnp.bfloat16),
        scratch_shapes=[pltpu.VMEM((depths * rows, 128), jnp.float32)],
        compiler_params=pltpu.CompilerParams(vmem_limit_bytes=60 << 20),
        cost_estimate=pl.CostEstimate(flops=2 * depths * total * rows * columns, bytes_accessed=14 << 20, transcendentals=0),
        name="fdf",
    )(kt, res.reshape(count, 2, tiles, rows // 2, total, 128))


def clean_tile(chans, pair, half, rows, data, peaks, t, spread, out_ref, oh, e4, ec, es, joint):
    groups = chans // 8
    stays, moves = pair * 2 + half, pair * 2 + 1 - half
    here = (lax.broadcasted_iota(jnp.int32, (8, 128), 1) < 64) == (half == 0)

    def merged(ref, base):
        kept = ref[pl.ds(base + stays, 8, rows), :]
        moved = ref[pl.ds(base + moves, 8, rows), :]
        return jnp.where(here, kept, pltpu.roll(moved, 64, 1))

    picks = merged(peaks, 0)
    lo = picks & (LOW - 1)
    hi = (picks >> 6) + LOW
    index = lax.broadcasted_iota(jnp.int32, (128, 128), 0)
    for j in range(NC):
        cols = slice(j * 128, (j + 1) * 128)
        hot = ((index == lo[j:j+1]) | (index == hi[j:j+1])).astype(jnp.bfloat16)
        oh[0:128, cols] = hot
        oh[128:256, cols] = hot
    e4[...] = jnp.dot(t[...], oh[...], preferred_element_type=jnp.float32)

    def join(g, _):
        for k in range(6):
            joint[0, g * 6 + k] = merged(data.at[0], (g * 6 + k) * (8 * rows))
            joint[1, g * 6 + k] = merged(data.at[1], (g * 6 + k) * (8 * rows))
        return 0

    lax.fori_loop(0, groups // 6, join, 0)

    def peak(g, acc):
        q, u = joint[0, g], joint[1, g]
        base = pl.multiple_of(g * 32, 32)
        out = []
        for j in range(NC):
            cols = slice(j * 128, (j + 1) * 128)
            cl, sl = e4[pl.ds(base, 8), cols], e4[pl.ds(base + 8, 8), cols]
            ch, sh = e4[pl.ds(base + 16, 8), cols], e4[pl.ds(base + 24, 8), cols]
            c = ch * cl - sh * sl
            s = sh * cl + ch * sl
            ec[g * NC + j] = c
            es[g * NC + j] = s
            out.append((acc[j][0] + (q * c + u * s), acc[j][1] + (u * c - q * s)))
        return tuple(out)

    zero = jnp.zeros((8, 128), jnp.float32)
    acc = lax.fori_loop(0, groups, peak, tuple((zero, zero) for _ in range(NC)))
    scale = 1.0 / chans
    vr = jnp.concatenate([jnp.sum(a[0], axis=0, keepdims=True) for a in acc], axis=0) * scale
    vi = jnp.concatenate([jnp.sum(a[1], axis=0, keepdims=True) for a in acc], axis=0) * scale
    comps = []
    for i in range(NC):
        cr = full(vr[i:i+1] * GAIN)
        ci = full(vi[i:i+1] * GAIN)
        comps.append((cr, ci))
        if i == NC - 1:
            break
        d = picks - picks[i:i+1]
        a = jnp.abs(d)
        alo, ahi = a & 127, a >> 7
        rr, ri = zero, zero
        for h in range(16):
            here = ahi == h
            rr = jnp.where(here, gather(full(spread[0, h:h+1, :]), alo), rr)
            ri = jnp.where(here, gather(full(spread[1, h:h+1, :]), alo), ri)
        ri = jnp.where(d < 0, -ri, ri)
        vr = vr - (cr * rr - ci * ri)
        vi = vi - (cr * ri + ci * rr)

    def model(pair, _):
        real, imag = [], []
        for part in range(2):
            g = pair * 2 + part
            q, u = joint[0, g], joint[1, g]
            mr, mi = zero, zero
            for j in range(NC):
                c, s = ec[g * NC + j], es[g * NC + j]
                cr, ci = comps[j]
                mr = mr + (cr * c - ci * s)
                mi = mi + (cr * s + ci * c)
            real.append(q - mr)
            imag.append(u - mi)
        out_ref[pl.ds(pl.multiple_of(pair * 16, 16), 16), :] = jnp.concatenate(real, axis=0).astype(jnp.bfloat16)
        out_ref[pl.ds(pl.multiple_of(chans + pair * 16, 16), 16), :] = jnp.concatenate(imag, axis=0).astype(jnp.bfloat16)
        return 0

    lax.fori_loop(0, groups // 2, model, 0)


def island_kernel(chans, stokes_ref, row_ref, peaks_ref, owner_ref, w_ref, out_ref, kt_ref, got_ref, last_ref,
                  raw, data, res, w, fit, sent, t, near, spread, kt, ck, sk, peaks, joint_peaks, oh, e4, ec, es, joint, chosen,
                  own, sa, ra, sn, rn, sf, rf, so, ow, op, sw, rw, sc, rc, sd, rd, od, ok):
    count, skies = lax.axis_size("freq"), lax.axis_size("sky")
    me = lax.axis_index("freq")
    sky = lax.axis_index("sky")
    x, z, core = sky // 8, sky // 2 % 4, sky % 2
    rows = stokes_ref.shape[2]
    tiles = stokes_ref.shape[3] // (count * 128)
    chunks = rows * tiles
    halfway = chunks // 2
    local = stokes_ref.shape[1]
    half = chans
    left, right, far = [lax.rem(me + k, count) for k in (count - 1, 1, 2)]

    def at_x(k):
        return {"sky": lax.rem(x + k, 4) * 8 + z * 2 + core}

    def at_z(k):
        return {"sky": x * 8 + lax.rem(z + k, 4) * 2 + core}

    other = {"sky": sky + 1 - 2 * core}

    barrier = pltpu.get_barrier_semaphore()
    for k in range(1, 4):
        pl.semaphore_signal(barrier, inc=1, device_id={"freq": lax.rem(me + k, count)}, device_id_type=MESH)

    def greet(k, _):
        pl.semaphore_signal(barrier, inc=1, device_id={"sky": lax.rem(sky + k, skies)}, device_id_type=MESH)
        return 0

    lax.fori_loop(1, skies, greet, 0)
    pl.semaphore_wait(barrier, count + skies - 2)

    def columns(owner, tile):
        return pl.ds(pl.multiple_of((owner * tiles + tile) * 128, 128), 128)

    def part(tile, k):
        peer = lax.rem(me + k, count)
        return pltpu.make_async_remote_copy(
            src_ref=stokes_ref.at[:, :, :, columns(peer, tile)], dst_ref=raw.at[tile, me],
            send_sem=sa.at[tile, k], recv_sem=ra.at[tile, k], device_id={"freq": peer}, device_id_type=MESH)

    def arrived(tile, k):
        source = lax.rem(me + count - k, count)
        return pltpu.make_async_remote_copy(
            src_ref=stokes_ref.at[:, :, :, columns(me, tile)], dst_ref=raw.at[tile, source],
            send_sem=sa.at[tile, k], recv_sem=ra.at[tile, k], device_id={"freq": source}, device_id_type=MESH)

    def kept(tile):
        return pltpu.make_async_copy(stokes_ref.at[:, :, :, columns(me, tile)], raw.at[tile, me], own.at[tile])

    for tile in range(tiles):
        kept(tile).start()
        for k in (1, 3, 2):
            part(tile, k).start()
    mine = pl.ds(pl.multiple_of(me * (tiles * 128), 128), tiles * 128)
    pltpu.make_async_copy(peaks_ref.at[:, :, mine], peaks, op).start()
    pltpu.make_async_copy(w_ref.at[0], w.at[x, z, core], ow).start()
    pltpu.make_async_copy(w_ref.at[0], w.at[x, z, core], ow).wait()

    def w_first(h, k, source=None):
        along_x = h == 0
        lines = pl.ds(h * half, half)
        piece = w.at[x, z, core, lines]
        if source is not None:
            piece = w.at[lax.rem(x + 4 - k, 4), z, core, lines] if along_x else w.at[x, lax.rem(z + 4 - k, 4), core, lines]
        return pltpu.make_async_remote_copy(
            src_ref=piece, dst_ref=piece, send_sem=sw.at[0, h, k], recv_sem=rw.at[0, h, k],
            device_id=at_x(k) if along_x else at_z(k), device_id_type=MESH)

    def w_second(h, k, source=None):
        along_x = h == 1
        lines = pl.ds(h * half, half)
        back = k if source is not None else 4
        if along_x:
            piece = w.at[lax.rem(x + 4 - back + (4 if back == 4 else 0), 4), :, core, lines]
        else:
            piece = w.at[:, lax.rem(z + 4 - back + (4 if back == 4 else 0), 4), core, lines]
        return pltpu.make_async_remote_copy(
            src_ref=piece, dst_ref=piece, send_sem=sw.at[1, h, k], recv_sem=rw.at[1, h, k],
            device_id=at_x(k) if along_x else at_z(k), device_id_type=MESH)

    def w_third(which):
        piece = w.at[:, :, which]
        return pltpu.make_async_remote_copy(
            src_ref=piece, dst_ref=piece, send_sem=sc, recv_sem=rc, device_id=other, device_id_type=MESH)

    for h in range(2):
        for k in range(1, 4):
            w_first(h, k).start()

    def slot(o, _):
        first, second = jnp.int32(-1), jnp.int32(-1)
        for b in reversed(range(owner_ref.shape[0])):
            hit = owner_ref[b] == o
            second = jnp.where(hit, first, second)
            first = jnp.where(hit, b, first)
        chosen[o * 2] = first
        chosen[o * 2 + 1] = second
        return 0

    lax.fori_loop(0, skies, slot, 0)
    make_tables(chans, row_ref, t, near, spread)

    def to_neighbour(c, way, source):
        return pltpu.make_async_remote_copy(
            src_ref=res.at[source, c], dst_ref=res.at[source, c],
            send_sem=sn.at[c, way], recv_sem=rn.at[c, way],
            device_id={"freq": right if way == 0 else left}, device_id_type=MESH)

    def onward(c, way, source):
        piece = res.at[source, c, pl.ds(way * half, half)]
        return pltpu.make_async_remote_copy(
            src_ref=piece, dst_ref=piece, send_sem=sf.at[c, way], recv_sem=rf.at[c, way],
            device_id={"freq": right if way == 0 else left}, device_id_type=MESH)

    def keep(c, source):
        return pltpu.make_async_copy(res.at[source, c], out_ref.at[source, c], so.at[c, source])

    def relay(c):
        to_neighbour(c, 0, left).wait_recv()
        onward(c, 0, left).start()
        keep(c, left).start()
        to_neighbour(c, 1, right).wait_recv()
        onward(c, 1, right).start()
        keep(c, right).start()

    def fit_chunk(source, c):
        part, tile, pair = c // halfway, c // 2 % tiles, c % 2
        b = pair * (2 * count * tiles) + source * tiles + tile
        after = b + count * tiles
        o, p = owner_ref[b], owner_ref[after]
        both = jnp.concatenate([w[o >> 3, (o >> 1) & 3, o & 1], w[p >> 3, (p >> 1) & 3, p & 1]], axis=1)
        value = lax.dot_general(res[source, c], both, (((0,), (0,)), ((), ())), preferred_element_type=jnp.float32)
        terms = value.shape[1] // 2
        fit[part, b] = value[:64, :terms].astype(jnp.bfloat16)
        fit[part, after] = value[64:, terms:].astype(jnp.bfloat16)

    def fit_some(sources, first, last):
        def some(c, _):
            for source in sources:
                fit_chunk(source, c)
            return 0
        lax.fori_loop(first, last, some, 0)

    def fit_far(first, last):
        def some(c, _):
            onward(c, 0, far).wait_recv()
            onward(c, 1, far).wait_recv()
            keep(c, far).start()
            fit_chunk(far, c)
            return 0
        lax.fori_loop(first, last, some, 0)

    def result(k, source):
        peer = lax.rem(sky + k, skies)
        return pltpu.make_async_remote_copy(
            src_ref=sent.at[peer], dst_ref=got_ref.at[source],
            send_sem=sd.at[k], recv_sem=rd.at[k], device_id={"sky": peer}, device_id_type=MESH)

    def kept_result():
        return pltpu.make_async_copy(sent.at[sky], got_ref.at[sky], od)

    def fill_slots(part, slots):
        def fill(o, _):
            for rank in range(2):
                b = chosen[o * 2 + rank]
                value = fit[part, jnp.maximum(b, 0)]
                slots[o, rank] = jnp.where(b >= 0, value, jnp.zeros_like(value))
            return 0

        lax.fori_loop(0, skies, fill, 0)

    def send_results():
        def send(k, _):
            result(k, sky).start()
            return 0

        fill_slots(0, sent)
        lax.fori_loop(1, skies, send, 0)
        kept_result().start()

    pltpu.make_async_copy(peaks_ref.at[:, :, mine], peaks, op).wait()

    def step(c, _):
        part, tile, pair = c // halfway, c // 2 % tiles, c % 2

        @pl.when((pair == 0) & (part == 0))
        def _():
            kept(tile).wait()
            for k in (1, 3, 2):
                arrived(tile, k).wait_recv()
            for source in range(count):
                for plane in range(2):
                    block = raw[tile, source, plane].reshape(local * rows, 128)
                    data[tile, plane, source * local * rows:(source + 1) * local * rows, :] = block.astype(jnp.float32)
            joint_peaks[tile] = peaks[:, :, pl.ds(pl.multiple_of(tile * 128, 128), 128)].reshape(NC * rows, 128)

        clean_tile(chans, pair, part, rows, data.at[tile], joint_peaks.at[tile], t, spread, res.at[me, c], oh, e4, ec, es, joint)
        to_neighbour(c, 0, me).start()
        to_neighbour(c, 1, me).start()
        keep(c, me).start()

        @pl.when(c >= LAG)
        def _():
            relay(c - LAG)

        @pl.when(c == 1)
        def _():
            for h in range(2):
                for k in range(1, 4):
                    w_first(h, k, True).wait_recv()
            for h in range(2):
                for k in range(1, 4):
                    w_second(h, k).start()
            make_synthesis(chans, row_ref, me * (kt.shape[0] // 2), kt, ck, sk)
            pltpu.make_async_copy(kt, kt_ref, ok).start()

        @pl.when(c == 4)
        def _():
            for h in range(2):
                for k in range(1, 4):
                    w_second(h, k, True).wait_recv()
            w_third(core).start()

        @pl.when(c == 5)
        def _():
            w_third(1 - core).wait_recv()
            fit_some((me,), 0, halfway)
            fit_some((left, right), 0, halfway - 1)

        @pl.when(c == 6)
        def _():
            fit_some((left, right), halfway - 1, halfway)
            fit_far(0, halfway)
            send_results()

        return 0

    lax.fori_loop(0, chunks, step, 0)
    fit_some((me,), halfway, chunks)
    relay(chunks - 2)
    fit_some((left, right), halfway, chunks - 1)
    relay(chunks - 1)
    fit_far(halfway, chunks - 1)
    fit_some((left, right), chunks - 1, chunks)
    fit_far(chunks - 1, chunks)
    fill_slots(1, last_ref)

    for tile in range(tiles):
        for k in (1, 3, 2):
            part(tile, k).wait_send()
    for h in range(2):
        for k in range(1, 4):
            w_first(h, k).wait_send()
            w_second(h, k).wait_send()
    w_third(core).wait_send()

    def finish(c, _):
        to_neighbour(c, 0, me).wait_send()
        to_neighbour(c, 1, me).wait_send()
        onward(c, 0, left).wait_send()
        onward(c, 1, right).wait_send()
        for source in (me, left, right, far):
            keep(c, source).wait()
        return 0

    lax.fori_loop(0, chunks, finish, 0)
    pltpu.make_async_copy(kt, kt_ref, ok).wait()
    kept_result().wait()

    def results(k, _):
        result(k, lax.rem(sky + skies - k, skies)).wait_recv()
        result(k, sky).wait_send()
        return 0

    lax.fori_loop(1, skies, results, 0)


def islands(stokes, lam2, peaks, owners, weights, freq_count, sky_count):
    chans, local, rows, columns = lam2.shape[0], stokes.shape[1], stokes.shape[2], stokes.shape[3]
    groups = chans // 8
    tiles = columns // (freq_count * 128)
    chunks = rows * tiles
    terms = weights.shape[2]
    depths = DEPTHS // freq_count
    dma = pltpu.SemaphoreType.DMA
    vmem = pl.BlockSpec(memory_space=pltpu.VMEM)
    smem = pl.BlockSpec(memory_space=pltpu.SMEM)
    hbm = pl.BlockSpec(memory_space=pl.ANY)
    f32, bf16 = jnp.float32, jnp.bfloat16
    return pl.pallas_call(
        functools.partial(island_kernel, chans),
        in_specs=[hbm, vmem, hbm, smem, hbm],
        out_specs=[hbm, hbm, hbm, vmem],
        out_shape=[
            jax.ShapeDtypeStruct((freq_count, chunks, 2 * chans, 128), bf16),
            jax.ShapeDtypeStruct((2 * depths, 2 * chans), bf16),
            jax.ShapeDtypeStruct((sky_count, 2, 64, terms), bf16),
            jax.ShapeDtypeStruct((sky_count, 2, 64, terms), bf16),
        ],
        scratch_shapes=[
            pltpu.VMEM((tiles, freq_count, 2, local, rows, 128), bf16),
            pltpu.VMEM((tiles, 2, chans * rows, 128), f32),
            pltpu.VMEM((freq_count, chunks, 2 * chans, 128), bf16),
            pltpu.VMEM((4, 4, 2, 2 * chans, terms), bf16),
            pltpu.VMEM((2, freq_count * chunks, 64, terms), bf16),
            pltpu.VMEM((sky_count, 2, 64, terms), bf16),
            pltpu.VMEM((4 * chans, 256), bf16),
            pltpu.VMEM((2, chans, 128), f32),
            pltpu.VMEM((2, 16, 128), f32),
            pltpu.VMEM((2 * depths, 2 * chans), bf16),
            pltpu.VMEM((LOW, 2 * chans), f32),
            pltpu.VMEM((LOW, 2 * chans), f32),
            pltpu.VMEM((NC, rows, tiles * 128), jnp.int32),
            pltpu.VMEM((tiles, NC * rows, 128), jnp.int32),
            pltpu.VMEM((256, NC * 128), bf16),
            pltpu.VMEM((4 * chans, NC * 128), f32),
            pltpu.VMEM((groups * NC, 8, 128), f32),
            pltpu.VMEM((groups * NC, 8, 128), f32),
            pltpu.VMEM((2, groups, 8, 128), f32),
            pltpu.SMEM((sky_count * 2,), jnp.int32),
            dma((tiles,)), dma((tiles, 4)), dma((tiles, 4)),
            dma((chunks, 2)), dma((chunks, 2)), dma((chunks, 2)), dma((chunks, 2)), dma((chunks, 4)),
            dma, dma, dma((2, 2, 4)), dma((2, 2, 4)), dma, dma,
            dma((sky_count,)), dma((sky_count,)), dma, dma,
        ],
        compiler_params=pltpu.CompilerParams(collective_id=0, has_side_effects=True, vmem_limit_bytes=60 << 20),
        cost_estimate=pl.CostEstimate(flops=6 << 32, bytes_accessed=24 << 20, transcendentals=0),
        name="islands",
    )(stokes, lam2.reshape(1, chans), peaks, owners, weights)


def shards(stokes, lam2, peaks, island_owner, fit_matrix):
    freq_count, sky_count = lax.axis_size("freq"), lax.axis_size("sky")
    res, kt, early, late = islands(stokes, lam2, peaks, island_owner[:, 0], fit_matrix, freq_count, sky_count)
    late = lax.all_to_all(late, "sky", split_axis=0, concat_axis=0, tiled=True)
    coefficients = jnp.concatenate([early, late], axis=2)
    return fdf(kt, res, stokes.shape[2]), coefficients.astype(jnp.float32)[None]


def solution(mesh):
    in_specs = (
        P(None, "freq", "sky", None),
        P(),
        P(None, "sky", None),
        P("sky", None),
        P("sky", None, "freq"),
    )
    out_specs = (P(None, "freq", "sky", None), P("sky", None, None, None, "freq"))
    return jax.shard_map(shards, mesh=mesh, in_specs=in_specs, out_specs=out_specs, check_vma=False)
```

```python
import functools
import jax
import jax.numpy as jnp
from jax import lax
from jax.sharding import PartitionSpec as P
from jax.experimental import pallas as pl
from jax.experimental.pallas import tpu as pltpu

NC = 8
DEPTHS = 2048
STEP = 2.5
BLK = 128
LAG = 2
MESH = pl.DeviceIdType.MESH
GAIN = 0.3
LOW = 64

def gather(x, idx):
    return jnp.take_along_axis(x, idx, axis=1, mode="promise_in_bounds")


def full(row):
    return jnp.broadcast_to(row, (8, 128))


def make_tables(chans, row_ref, t, near, spread):
    mean = jnp.sum(row_ref[...], axis=1, keepdims=True) / chans
    along = jnp.broadcast_to(row_ref[...] - mean, (8, chans))
    place = lax.broadcasted_iota(jnp.int32, (8, chans), 1) - lax.broadcasted_iota(jnp.int32, (8, chans), 0)
    lane = lax.broadcasted_iota(jnp.int32, (8, 128), 1)
    low = lane < LOW
    depth = jnp.where(low, lane, (lane - LOW) * LOW - DEPTHS // 2).astype(jnp.float32) * STEP
    plain = lane.astype(jnp.float32) * STEP

    def rows(g, _):
        twice = 2.0 * jnp.sum(jnp.where(place == g * 8, along, 0.0), axis=1, keepdims=True)
        angle = twice * depth
        parts = []
        for mask in (low, ~low):
            for value in (jnp.cos(angle), jnp.sin(angle)):
                value = jnp.where(mask, value, 0.0)
                top = value.astype(jnp.bfloat16)
                parts.append(jnp.concatenate([top, (value - top.astype(jnp.float32)).astype(jnp.bfloat16)], axis=1))
        t[pl.ds(pl.multiple_of(g * 32, 32), 32), :] = jnp.concatenate(parts, axis=0)
        angle = twice * plain
        near[0, pl.ds(pl.multiple_of(g * 8, 8), 8), :] = jnp.cos(angle)
        near[1, pl.ds(pl.multiple_of(g * 8, 8), 8), :] = jnp.sin(angle)
        return 0

    lax.fori_loop(0, chans // 8, rows, 0)
    twice = 2.0 * (row_ref[...] - mean)
    angle = twice * (lax.broadcasted_iota(jnp.int32, (16, chans), 0).astype(jnp.float32) * (128 * STEP))
    cosine, sine = jnp.cos(angle), jnp.sin(angle)
    dot = functools.partial(jnp.dot, precision=lax.Precision.HIGHEST, preferred_element_type=jnp.float32)
    spread[0] = (dot(cosine, near[0]) - dot(sine, near[1])) / chans
    spread[1] = -(dot(sine, near[0]) + dot(cosine, near[1])) / chans


def make_synthesis(chans, row_ref, first, kt, ck, sk):
    total = 2 * chans
    depths = kt.shape[0] // 2
    mean = jnp.sum(row_ref[...], axis=1, keepdims=True) / chans
    twice = 2.0 * (row_ref[...] - mean)
    twice = jnp.concatenate([twice, twice], axis=1)
    fine = twice * (lax.broadcasted_iota(jnp.int32, (LOW, total), 0).astype(jnp.float32) * STEP)
    ck[...] = jnp.cos(fine)
    sk[...] = jnp.sin(fine)
    steps = lax.broadcasted_iota(jnp.int32, (8, total), 0) * LOW + (first - DEPTHS // 2)
    coarse = twice * (steps.astype(jnp.float32) * STEP)
    cosine, sine = jnp.cos(coarse), jnp.sin(coarse)
    is_q = lax.broadcasted_iota(jnp.int32, (16, total), 1) < chans
    for h in range(depths // LOW):
        ch, sh = cosine[h:h+1], sine[h:h+1]
        for l in range(0, LOW, 16):
            cl, sl = ck[l:l+16, :], sk[l:l+16, :]
            c = (ch * cl - sh * sl) / chans
            s = (sh * cl + ch * sl) / chans
            at = h * LOW + l
            kt[at:at+16, :] = jnp.where(is_q, c, s).astype(jnp.bfloat16)
            kt[depths+at:depths+at+16, :] = jnp.where(is_q, -s, c).astype(jnp.bfloat16)


def fdf_kernel(k_ref, res_ref, out_ref, mixed):
    rows, depths = out_ref.shape[2], k_ref.shape[0]
    for pair in range(rows // 2):
        a, b = res_ref[0, 0, 0, pair], res_ref[0, 1, 0, pair]
        block = jnp.concatenate([a[:, :64], b[:, :64], a[:, 64:], b[:, 64:]], axis=1)
        for first in range(0, depths, 256):
            part = jnp.dot(k_ref[first:first + 256, :], block, preferred_element_type=jnp.float32)
            for row in range(2):
                mixed[pl.ds(first * rows + pair * 2 + row, 256, rows), :] = part[:, row * 128:(row + 1) * 128]
    out_ref[...] = mixed[...].astype(jnp.bfloat16).reshape(out_ref.shape)


def fdf(kt, res, rows):
    count, chunks, total, _ = res.shape
    tiles = chunks // rows
    depths = kt.shape[0]
    columns = count * tiles * 128
    return pl.pallas_call(
        fdf_kernel,
        grid=(count * tiles,),
        in_specs=[
            pl.BlockSpec((depths, total), lambda i: (0, 0)),
            pl.BlockSpec((1, 2, 1, rows // 2, total, 128), lambda i: (i // tiles, 0, i % tiles, 0, 0, 0)),
        ],
        out_specs=pl.BlockSpec((2, depths // 2, rows, 128), lambda i: (0, 0, 0, i)),
        out_shape=jax.ShapeDtypeStruct((2, depths // 2, rows, columns), jnp.bfloat16),
        scratch_shapes=[pltpu.VMEM((depths * rows, 128), jnp.float32)],
        compiler_params=pltpu.CompilerParams(vmem_limit_bytes=60 << 20),
        cost_estimate=pl.CostEstimate(flops=2 * depths * total * rows * columns, bytes_accessed=14 << 20, transcendentals=0),
        name="fdf",
    )(kt, res.reshape(count, 2, tiles, rows // 2, total, 128))


def clean_tile(chans, pair, half, rows, data, peaks, t, spread, out_ref, oh, e4, ec, es, joint):
    groups = chans // 8
    stays, moves = pair * 2 + half, pair * 2 + 1 - half
    here = (lax.broadcasted_iota(jnp.int32, (8, 128), 1) < 64) == (half == 0)

    def merged(ref, base):
        kept = ref[pl.ds(base + stays, 8, rows), :]
        moved = ref[pl.ds(base + moves, 8, rows), :]
        return jnp.where(here, kept, pltpu.roll(moved, 64, 1))

    picks = merged(peaks, 0)
    lo = picks & (LOW - 1)
    hi = (picks >> 6) + LOW
    index = lax.broadcasted_iota(jnp.int32, (128, 128), 0)
    for j in range(NC):
        cols = slice(j * 128, (j + 1) * 128)
        hot = ((index == lo[j:j+1]) | (index == hi[j:j+1])).astype(jnp.bfloat16)
        oh[0:128, cols] = hot
        oh[128:256, cols] = hot
    e4[...] = jnp.dot(t[...], oh[...], preferred_element_type=jnp.float32)

    def join(g, _):
        for k in range(6):
            joint[0, g * 6 + k] = merged(data.at[0], (g * 6 + k) * (8 * rows))
            joint[1, g * 6 + k] = merged(data.at[1], (g * 6 + k) * (8 * rows))
        return 0

    lax.fori_loop(0, groups // 6, join, 0)

    def peak(g, acc):
        q, u = joint[0, g], joint[1, g]
        base = pl.multiple_of(g * 32, 32)
        out = []
        for j in range(NC):
            cols = slice(j * 128, (j + 1) * 128)
            cl, sl = e4[pl.ds(base, 8), cols], e4[pl.ds(base + 8, 8), cols]
            ch, sh = e4[pl.ds(base + 16, 8), cols], e4[pl.ds(base + 24, 8), cols]
            c = ch * cl - sh * sl
            s = sh * cl + ch * sl
            ec[g * NC + j] = c
            es[g * NC + j] = s
            out.append((acc[j][0] + (q * c + u * s), acc[j][1] + (u * c - q * s)))
        return tuple(out)

    zero = jnp.zeros((8, 128), jnp.float32)
    acc = lax.fori_loop(0, groups, peak, tuple((zero, zero) for _ in range(NC)))
    scale = 1.0 / chans
    vr = jnp.concatenate([jnp.sum(a[0], axis=0, keepdims=True) for a in acc], axis=0) * scale
    vi = jnp.concatenate([jnp.sum(a[1], axis=0, keepdims=True) for a in acc], axis=0) * scale
    comps = []
    for i in range(NC):
        cr = full(vr[i:i+1] * GAIN)
        ci = full(vi[i:i+1] * GAIN)
        comps.append((cr, ci))
        if i == NC - 1:
            break
        d = picks - picks[i:i+1]
        a = jnp.abs(d)
        alo, ahi = a & 127, a >> 7
        rr, ri = zero, zero
        for h in range(16):
            here = ahi == h
            rr = jnp.where(here, gather(full(spread[0, h:h+1, :]), alo), rr)
            ri = jnp.where(here, gather(full(spread[1, h:h+1, :]), alo), ri)
        ri = jnp.where(d < 0, -ri, ri)
        vr = vr - (cr * rr - ci * ri)
        vi = vi - (cr * ri + ci * rr)

    def model(pair, _):
        real, imag = [], []
        for part in range(2):
            g = pair * 2 + part
            q, u = joint[0, g], joint[1, g]
            mr, mi = zero, zero
            for j in range(NC):
                c, s = ec[g * NC + j], es[g * NC + j]
                cr, ci = comps[j]
                mr = mr + (cr * c - ci * s)
                mi = mi + (cr * s + ci * c)
            real.append(q - mr)
            imag.append(u - mi)
        out_ref[pl.ds(pl.multiple_of(pair * 16, 16), 16), :] = jnp.concatenate(real, axis=0).astype(jnp.bfloat16)
        out_ref[pl.ds(pl.multiple_of(chans + pair * 16, 16), 16), :] = jnp.concatenate(imag, axis=0).astype(jnp.bfloat16)
        return 0

    lax.fori_loop(0, groups // 2, model, 0)


def island_kernel(chans, stokes_ref, row_ref, peaks_ref, owner_ref, w_ref, out_ref, kt_ref, got_ref, last_ref,
                  raw, data, res, w, fit, sent, t, near, spread, kt, ck, sk, peaks, joint_peaks, oh, e4, ec, es, joint, chosen,
                  own, sa, ra, sn, rn, sf, rf, so, ow, op, sw, rw, sc, rc, sd, rd, od, ok):
    count, skies = lax.axis_size("freq"), lax.axis_size("sky")
    me = lax.axis_index("freq")
    sky = lax.axis_index("sky")
    x, z, core = sky // 8, sky // 2 % 4, sky % 2
    rows = stokes_ref.shape[2]
    tiles = stokes_ref.shape[3] // (count * 128)
    chunks = rows * tiles
    halfway = chunks // 2
    local = stokes_ref.shape[1]
    half = chans
    left, right, far = [lax.rem(me + k, count) for k in (count - 1, 1, 2)]

    def at_x(k):
        return {"sky": lax.rem(x + k, 4) * 8 + z * 2 + core}

    def at_z(k):
        return {"sky": x * 8 + lax.rem(z + k, 4) * 2 + core}

    other = {"sky": sky + 1 - 2 * core}

    barrier = pltpu.get_barrier_semaphore()
    for k in range(1, 4):
        pl.semaphore_signal(barrier, inc=1, device_id={"freq": lax.rem(me + k, count)}, device_id_type=MESH)

    def greet(k, _):
        pl.semaphore_signal(barrier, inc=1, device_id={"sky": lax.rem(sky + k, skies)}, device_id_type=MESH)
        return 0

    lax.fori_loop(1, skies, greet, 0)
    pl.semaphore_wait(barrier, count + skies - 2)

    def columns(owner, tile):
        return pl.ds(pl.multiple_of((owner * tiles + tile) * 128, 128), 128)

    def part(tile, k):
        peer = lax.rem(me + k, count)
        return pltpu.make_async_remote_copy(
            src_ref=stokes_ref.at[:, :, :, columns(peer, tile)], dst_ref=raw.at[tile, me],
            send_sem=sa.at[tile, k], recv_sem=ra.at[tile, k], device_id={"freq": peer}, device_id_type=MESH)

    def arrived(tile, k):
        source = lax.rem(me + count - k, count)
        return pltpu.make_async_remote_copy(
            src_ref=stokes_ref.at[:, :, :, columns(me, tile)], dst_ref=raw.at[tile, source],
            send_sem=sa.at[tile, k], recv_sem=ra.at[tile, k], device_id={"freq": source}, device_id_type=MESH)

    def kept(tile):
        return pltpu.make_async_copy(stokes_ref.at[:, :, :, columns(me, tile)], raw.at[tile, me], own.at[tile])

    for tile in range(tiles):
        kept(tile).start()
        for k in (1, 3, 2):
            part(tile, k).start()
    mine = pl.ds(pl.multiple_of(me * (tiles * 128), 128), tiles * 128)
    pltpu.make_async_copy(peaks_ref.at[:, :, mine], peaks, op).start()
    pltpu.make_async_copy(w_ref.at[0], w.at[x, z, core], ow).start()
    pltpu.make_async_copy(w_ref.at[0], w.at[x, z, core], ow).wait()

    def w_first(h, k, source=None):
        along_x = h == 0
        lines = pl.ds(h * half, half)
        piece = w.at[x, z, core, lines]
        if source is not None:
            piece = w.at[lax.rem(x + 4 - k, 4), z, core, lines] if along_x else w.at[x, lax.rem(z + 4 - k, 4), core, lines]
        return pltpu.make_async_remote_copy(
            src_ref=piece, dst_ref=piece, send_sem=sw.at[0, h, k], recv_sem=rw.at[0, h, k],
            device_id=at_x(k) if along_x else at_z(k), device_id_type=MESH)

    def w_second(h, k, source=None):
        along_x = h == 1
        lines = pl.ds(h * half, half)
        back = k if source is not None else 4
        if along_x:
            piece = w.at[lax.rem(x + 4 - back + (4 if back == 4 else 0), 4), :, core, lines]
        else:
            piece = w.at[:, lax.rem(z + 4 - back + (4 if back == 4 else 0), 4), core, lines]
        return pltpu.make_async_remote_copy(
            src_ref=piece, dst_ref=piece, send_sem=sw.at[1, h, k], recv_sem=rw.at[1, h, k],
            device_id=at_x(k) if along_x else at_z(k), device_id_type=MESH)

    def w_third(which):
        piece = w.at[:, :, which]
        return pltpu.make_async_remote_copy(
            src_ref=piece, dst_ref=piece, send_sem=sc, recv_sem=rc, device_id=other, device_id_type=MESH)

    for h in range(2):
        for k in range(1, 4):
            w_first(h, k).start()

    def slot(o, _):
        first, second = jnp.int32(-1), jnp.int32(-1)
        for b in reversed(range(owner_ref.shape[0])):
            hit = owner_ref[b] == o
            second = jnp.where(hit, first, second)
            first = jnp.where(hit, b, first)
        chosen[o * 2] = first
        chosen[o * 2 + 1] = second
        return 0

    lax.fori_loop(0, skies, slot, 0)
    make_tables(chans, row_ref, t, near, spread)

    def to_neighbour(c, way, source):
        return pltpu.make_async_remote_copy(
            src_ref=res.at[source, c], dst_ref=res.at[source, c],
            send_sem=sn.at[c, way], recv_sem=rn.at[c, way],
            device_id={"freq": right if way == 0 else left}, device_id_type=MESH)

    def onward(c, way, source):
        piece = res.at[source, c, pl.ds(way * half, half)]
        return pltpu.make_async_remote_copy(
            src_ref=piece, dst_ref=piece, send_sem=sf.at[c, way], recv_sem=rf.at[c, way],
            device_id={"freq": right if way == 0 else left}, device_id_type=MESH)

    def keep(c, source):
        return pltpu.make_async_copy(res.at[source, c], out_ref.at[source, c], so.at[c, source])

    def relay(c):
        to_neighbour(c, 0, left).wait_recv()
        onward(c, 0, left).start()
        keep(c, left).start()
        to_neighbour(c, 1, right).wait_recv()
        onward(c, 1, right).start()
        keep(c, right).start()

    def fit_chunk(source, c):
        part, tile, pair = c // halfway, c // 2 % tiles, c % 2
        b = pair * (2 * count * tiles) + source * tiles + tile
        after = b + count * tiles
        o, p = owner_ref[b], owner_ref[after]
        both = jnp.concatenate([w[o >> 3, (o >> 1) & 3, o & 1], w[p >> 3, (p >> 1) & 3, p & 1]], axis=1)
        value = lax.dot_general(res[source, c], both, (((0,), (0,)), ((), ())), preferred_element_type=jnp.float32)
        terms = value.shape[1] // 2
        fit[part, b] = value[:64, :terms].astype(jnp.bfloat16)
        fit[part, after] = value[64:, terms:].astype(jnp.bfloat16)

    def fit_some(sources, first, last):
        def some(c, _):
            for source in sources:
                fit_chunk(source, c)
            return 0
        lax.fori_loop(first, last, some, 0)

    def fit_far(first, last):
        def some(c, _):
            onward(c, 0, far).wait_recv()
            onward(c, 1, far).wait_recv()
            keep(c, far).start()
            fit_chunk(far, c)
            return 0
        lax.fori_loop(first, last, some, 0)

    def result(k, source):
        peer = lax.rem(sky + k, skies)
        return pltpu.make_async_remote_copy(
            src_ref=sent.at[peer], dst_ref=got_ref.at[source],
            send_sem=sd.at[k], recv_sem=rd.at[k], device_id={"sky": peer}, device_id_type=MESH)

    def kept_result():
        return pltpu.make_async_copy(sent.at[sky], got_ref.at[sky], od)

    def fill_slots(part, slots):
        def fill(o, _):
            for rank in range(2):
                b = chosen[o * 2 + rank]
                value = fit[part, jnp.maximum(b, 0)]
                slots[o, rank] = jnp.where(b >= 0, value, jnp.zeros_like(value))
            return 0

        lax.fori_loop(0, skies, fill, 0)

    def send_results(first, last):
        def send(k, _):
            result(lax.rem(k * 13, skies), sky).start()
            return 0

        lax.fori_loop(first, last, send, 0)

    pltpu.make_async_copy(peaks_ref.at[:, :, mine], peaks, op).wait()

    def step(c, _):
        part, tile, pair = c // halfway, c // 2 % tiles, c % 2

        @pl.when((pair == 0) & (part == 0))
        def _():
            kept(tile).wait()
            for k in (1, 3, 2):
                arrived(tile, k).wait_recv()
            for source in range(count):
                for plane in range(2):
                    block = raw[tile, source, plane].reshape(local * rows, 128)
                    data[tile, plane, source * local * rows:(source + 1) * local * rows, :] = block.astype(jnp.float32)
            joint_peaks[tile] = peaks[:, :, pl.ds(pl.multiple_of(tile * 128, 128), 128)].reshape(NC * rows, 128)

        clean_tile(chans, pair, part, rows, data.at[tile], joint_peaks.at[tile], t, spread, res.at[me, c], oh, e4, ec, es, joint)
        to_neighbour(c, 0, me).start()
        to_neighbour(c, 1, me).start()
        keep(c, me).start()

        @pl.when(c >= LAG)
        def _():
            relay(c - LAG)

        @pl.when(c == 1)
        def _():
            for h in range(2):
                for k in range(1, 4):
                    w_first(h, k, True).wait_recv()
            for h in range(2):
                for k in range(1, 4):
                    w_second(h, k).start()
            make_synthesis(chans, row_ref, me * (kt.shape[0] // 2), kt, ck, sk)
            pltpu.make_async_copy(kt, kt_ref, ok).start()

        @pl.when(c == 4)
        def _():
            for h in range(2):
                for k in range(1, 4):
                    w_second(h, k, True).wait_recv()
            w_third(core).start()

        @pl.when(c == 5)
        def _():
            w_third(1 - core).wait_recv()
            fit_some((me,), 0, halfway)
            fit_some((left, right), 0, halfway - 1)

        @pl.when(c == 6)
        def _():
            fit_some((left, right), halfway - 1, halfway)
            fit_far(0, halfway)
            fill_slots(0, sent)
            kept_result().start()
            send_results(1, 8)

        @pl.when(c == 7)
        def _():
            send_results(8, 16)

        return 0

    lax.fori_loop(0, chunks, step, 0)
    fit_some((me,), halfway, chunks)
    send_results(16, 24)
    relay(chunks - 2)
    fit_some((left, right), halfway, chunks - 1)
    send_results(24, 28)
    relay(chunks - 1)
    send_results(28, skies)
    fit_far(halfway, chunks - 1)
    fit_some((left, right), chunks - 1, chunks)
    fit_far(chunks - 1, chunks)
    fill_slots(1, last_ref)

    for tile in range(tiles):
        for k in (1, 3, 2):
            part(tile, k).wait_send()
    for h in range(2):
        for k in range(1, 4):
            w_first(h, k).wait_send()
            w_second(h, k).wait_send()
    w_third(core).wait_send()

    def finish(c, _):
        to_neighbour(c, 0, me).wait_send()
        to_neighbour(c, 1, me).wait_send()
        onward(c, 0, left).wait_send()
        onward(c, 1, right).wait_send()
        for source in (me, left, right, far):
            keep(c, source).wait()
        return 0

    lax.fori_loop(0, chunks, finish, 0)
    pltpu.make_async_copy(kt, kt_ref, ok).wait()
    kept_result().wait()

    def results(k, _):
        result(k, lax.rem(sky + skies - k, skies)).wait_recv()
        result(k, sky).wait_send()
        return 0

    lax.fori_loop(1, skies, results, 0)


def islands(stokes, lam2, peaks, owners, weights, freq_count, sky_count):
    chans, local, rows, columns = lam2.shape[0], stokes.shape[1], stokes.shape[2], stokes.shape[3]
    groups = chans // 8
    tiles = columns // (freq_count * 128)
    chunks = rows * tiles
    terms = weights.shape[2]
    depths = DEPTHS // freq_count
    dma = pltpu.SemaphoreType.DMA
    vmem = pl.BlockSpec(memory_space=pltpu.VMEM)
    smem = pl.BlockSpec(memory_space=pltpu.SMEM)
    hbm = pl.BlockSpec(memory_space=pl.ANY)
    f32, bf16 = jnp.float32, jnp.bfloat16
    return pl.pallas_call(
        functools.partial(island_kernel, chans),
        in_specs=[hbm, vmem, hbm, smem, hbm],
        out_specs=[hbm, hbm, hbm, vmem],
        out_shape=[
            jax.ShapeDtypeStruct((freq_count, chunks, 2 * chans, 128), bf16),
            jax.ShapeDtypeStruct((2 * depths, 2 * chans), bf16),
            jax.ShapeDtypeStruct((sky_count, 2, 64, terms), bf16),
            jax.ShapeDtypeStruct((sky_count, 2, 64, terms), bf16),
        ],
        scratch_shapes=[
            pltpu.VMEM((tiles, freq_count, 2, local, rows, 128), bf16),
            pltpu.VMEM((tiles, 2, chans * rows, 128), f32),
            pltpu.VMEM((freq_count, chunks, 2 * chans, 128), bf16),
            pltpu.VMEM((4, 4, 2, 2 * chans, terms), bf16),
            pltpu.VMEM((2, freq_count * chunks, 64, terms), bf16),
            pltpu.VMEM((sky_count, 2, 64, terms), bf16),
            pltpu.VMEM((4 * chans, 256), bf16),
            pltpu.VMEM((2, chans, 128), f32),
            pltpu.VMEM((2, 16, 128), f32),
            pltpu.VMEM((2 * depths, 2 * chans), bf16),
            pltpu.VMEM((LOW, 2 * chans), f32),
            pltpu.VMEM((LOW, 2 * chans), f32),
            pltpu.VMEM((NC, rows, tiles * 128), jnp.int32),
            pltpu.VMEM((tiles, NC * rows, 128), jnp.int32),
            pltpu.VMEM((256, NC * 128), bf16),
            pltpu.VMEM((4 * chans, NC * 128), f32),
            pltpu.VMEM((groups * NC, 8, 128), f32),
            pltpu.VMEM((groups * NC, 8, 128), f32),
            pltpu.VMEM((2, groups, 8, 128), f32),
            pltpu.SMEM((sky_count * 2,), jnp.int32),
            dma((tiles,)), dma((tiles, 4)), dma((tiles, 4)),
            dma((chunks, 2)), dma((chunks, 2)), dma((chunks, 2)), dma((chunks, 2)), dma((chunks, 4)),
            dma, dma, dma((2, 2, 4)), dma((2, 2, 4)), dma, dma,
            dma((sky_count,)), dma((sky_count,)), dma, dma,
        ],
        compiler_params=pltpu.CompilerParams(collective_id=0, has_side_effects=True, vmem_limit_bytes=60 << 20),
        cost_estimate=pl.CostEstimate(flops=6 << 32, bytes_accessed=24 << 20, transcendentals=0),
        name="islands",
    )(stokes, lam2.reshape(1, chans), peaks, owners, weights)


def shards(stokes, lam2, peaks, island_owner, fit_matrix):
    freq_count, sky_count = lax.axis_size("freq"), lax.axis_size("sky")
    res, kt, early, late = islands(stokes, lam2, peaks, island_owner[:, 0], fit_matrix, freq_count, sky_count)
    late = lax.all_to_all(late, "sky", split_axis=0, concat_axis=0, tiled=True)
    coefficients = jnp.concatenate([early, late], axis=2)
    return fdf(kt, res, stokes.shape[2]), coefficients.astype(jnp.float32)[None]


def solution(mesh):
    in_specs = (
        P(None, "freq", "sky", None),
        P(),
        P(None, "sky", None),
        P("sky", None),
        P("sky", None, "freq"),
    )
    out_specs = (P(None, "freq", "sky", None), P("sky", None, None, None, "freq"))
    return jax.shard_map(shards, mesh=mesh, in_specs=in_specs, out_specs=out_specs, check_vma=False)
```

```python
import functools
import jax
import jax.numpy as jnp
from jax import lax
from jax.sharding import PartitionSpec as P
from jax.experimental import pallas as pl
from jax.experimental.pallas import tpu as pltpu

NC = 8
DEPTHS = 2048
STEP = 2.5
BLK = 128
LAG = 2
MESH = pl.DeviceIdType.MESH
GAIN = 0.3
LOW = 64

def gather(x, idx):
    return jnp.take_along_axis(x, idx, axis=1, mode="promise_in_bounds")


def full(row):
    return jnp.broadcast_to(row, (8, 128))


def make_tables(chans, row_ref, t, near, spread):
    mean = jnp.sum(row_ref[...].reshape(1, chans), axis=1, keepdims=True) / chans
    along = jnp.broadcast_to(row_ref[...].reshape(1, chans) - mean, (8, chans))
    place = lax.broadcasted_iota(jnp.int32, (8, chans), 1) - lax.broadcasted_iota(jnp.int32, (8, chans), 0)
    lane = lax.broadcasted_iota(jnp.int32, (8, 128), 1)
    low = lane < LOW
    depth = jnp.where(low, lane, (lane - LOW) * LOW - DEPTHS // 2).astype(jnp.float32) * STEP
    plain = lane.astype(jnp.float32) * STEP

    def rows(g, _):
        twice = 2.0 * jnp.sum(jnp.where(place == g * 8, along, 0.0), axis=1, keepdims=True)
        angle = twice * depth
        parts = []
        for mask in (low, ~low):
            for value in (jnp.cos(angle), jnp.sin(angle)):
                value = jnp.where(mask, value, 0.0)
                top = value.astype(jnp.bfloat16)
                parts.append(jnp.concatenate([top, (value - top.astype(jnp.float32)).astype(jnp.bfloat16)], axis=1))
        t[pl.ds(pl.multiple_of(g * 32, 32), 32), :] = jnp.concatenate(parts, axis=0)
        angle = twice * plain
        near[0, pl.ds(pl.multiple_of(g * 8, 8), 8), :] = jnp.cos(angle)
        near[1, pl.ds(pl.multiple_of(g * 8, 8), 8), :] = jnp.sin(angle)
        return 0

    lax.fori_loop(0, chans // 8, rows, 0)
    twice = 2.0 * (row_ref[...].reshape(1, chans) - mean)
    angle = twice * (lax.broadcasted_iota(jnp.int32, (16, chans), 0).astype(jnp.float32) * (128 * STEP))
    cosine, sine = jnp.cos(angle), jnp.sin(angle)
    dot = functools.partial(jnp.dot, precision=lax.Precision.HIGHEST, preferred_element_type=jnp.float32)
    spread[0] = (dot(cosine, near[0]) - dot(sine, near[1])) / chans
    spread[1] = -(dot(sine, near[0]) + dot(cosine, near[1])) / chans


def make_synthesis(chans, row_ref, first, kt, ck, sk):
    total = 2 * chans
    depths = kt.shape[0] // 2
    mean = jnp.sum(row_ref[...].reshape(1, chans), axis=1, keepdims=True) / chans
    twice = 2.0 * (row_ref[...].reshape(1, chans) - mean)
    twice = jnp.concatenate([twice, twice], axis=1)
    fine = twice * (lax.broadcasted_iota(jnp.int32, (LOW, total), 0).astype(jnp.float32) * STEP)
    ck[...] = jnp.cos(fine)
    sk[...] = jnp.sin(fine)
    steps = lax.broadcasted_iota(jnp.int32, (8, total), 0) * LOW + (first - DEPTHS // 2)
    coarse = twice * (steps.astype(jnp.float32) * STEP)
    cosine, sine = jnp.cos(coarse), jnp.sin(coarse)
    is_q = lax.broadcasted_iota(jnp.int32, (16, total), 1) < chans
    for h in range(depths // LOW):
        ch, sh = cosine[h:h+1], sine[h:h+1]
        for l in range(0, LOW, 16):
            cl, sl = ck[l:l+16, :], sk[l:l+16, :]
            c = (ch * cl - sh * sl) / chans
            s = (sh * cl + ch * sl) / chans
            at = h * LOW + l
            kt[at:at+16, :] = jnp.where(is_q, c, s).astype(jnp.bfloat16)
            kt[depths+at:depths+at+16, :] = jnp.where(is_q, -s, c).astype(jnp.bfloat16)


def fdf_kernel(k_ref, res_ref, out_ref, mixed):
    rows, depths = out_ref.shape[2], k_ref.shape[0]
    for pair in range(rows // 2):
        a, b = res_ref[0, 0, 0, pair], res_ref[0, 1, 0, pair]
        block = jnp.concatenate([a[:, :64], b[:, :64], a[:, 64:], b[:, 64:]], axis=1)
        for first in range(0, depths, 256):
            part = jnp.dot(k_ref[first:first + 256, :], block, preferred_element_type=jnp.float32)
            for row in range(2):
                mixed[pl.ds(first * rows + pair * 2 + row, 256, rows), :] = part[:, row * 128:(row + 1) * 128]
    out_ref[...] = mixed[...].astype(jnp.bfloat16).reshape(out_ref.shape)


def fdf(kt, res, rows):
    count, chunks, total, _ = res.shape
    tiles = chunks // rows
    depths = kt.shape[0]
    columns = count * tiles * 128
    return pl.pallas_call(
        fdf_kernel,
        grid=(count * tiles,),
        in_specs=[
            pl.BlockSpec((depths, total), lambda i: (0, 0)),
            pl.BlockSpec((1, 2, 1, rows // 2, total, 128), lambda i: (i // tiles, 0, i % tiles, 0, 0, 0)),
        ],
        out_specs=pl.BlockSpec((2, depths // 2, rows, 128), lambda i: (0, 0, 0, i)),
        out_shape=jax.ShapeDtypeStruct((2, depths // 2, rows, columns), jnp.bfloat16),
        scratch_shapes=[pltpu.VMEM((depths * rows, 128), jnp.float32)],
        compiler_params=pltpu.CompilerParams(vmem_limit_bytes=48 << 20),
        cost_estimate=pl.CostEstimate(flops=2 * depths * total * rows * columns, bytes_accessed=14 << 20, transcendentals=0),
        name="fdf",
    )(kt, res.reshape(count, 2, tiles, rows // 2, total, 128))


def clean_tile(chans, pair, half, rows, data, peaks, t, spread, out_ref, oh, e4, ec, es, joint):
    groups = chans // 8
    stays, moves = pair * 2 + half, pair * 2 + 1 - half
    here = (lax.broadcasted_iota(jnp.int32, (8, 128), 1) < 64) == (half == 0)

    def merged(ref, base):
        kept = ref[pl.ds(base + stays, 8, rows), :]
        moved = ref[pl.ds(base + moves, 8, rows), :]
        return jnp.where(here, kept, pltpu.roll(moved, 64, 1))

    picks = merged(peaks, 0)
    lo = picks & (LOW - 1)
    hi = (picks >> 6) + LOW
    index = lax.broadcasted_iota(jnp.int32, (128, 128), 0)
    for j in range(NC):
        cols = slice(j * 128, (j + 1) * 128)
        hot = ((index == lo[j:j+1]) | (index == hi[j:j+1])).astype(jnp.bfloat16)
        oh[0:128, cols] = hot
        oh[128:256, cols] = hot
    e4[...] = jnp.dot(t[...], oh[...], preferred_element_type=jnp.float32)

    def join(g, _):
        for k in range(6):
            joint[0, g * 6 + k] = merged(data.at[0], (g * 6 + k) * (8 * rows))
            joint[1, g * 6 + k] = merged(data.at[1], (g * 6 + k) * (8 * rows))
        return 0

    lax.fori_loop(0, groups // 6, join, 0)

    def peak(g, acc):
        q, u = joint[0, g], joint[1, g]
        base = pl.multiple_of(g * 32, 32)
        out = []
        for j in range(NC):
            cols = slice(j * 128, (j + 1) * 128)
            cl, sl = e4[pl.ds(base, 8), cols], e4[pl.ds(base + 8, 8), cols]
            ch, sh = e4[pl.ds(base + 16, 8), cols], e4[pl.ds(base + 24, 8), cols]
            c = ch * cl - sh * sl
            s = sh * cl + ch * sl
            ec[g * NC + j] = c
            es[g * NC + j] = s
            out.append((acc[j][0] + (q * c + u * s), acc[j][1] + (u * c - q * s)))
        return tuple(out)

    zero = jnp.zeros((8, 128), jnp.float32)
    acc = lax.fori_loop(0, groups, peak, tuple((zero, zero) for _ in range(NC)))
    scale = 1.0 / chans
    vr = jnp.concatenate([jnp.sum(a[0], axis=0, keepdims=True) for a in acc], axis=0) * scale
    vi = jnp.concatenate([jnp.sum(a[1], axis=0, keepdims=True) for a in acc], axis=0) * scale
    comps = []
    for i in range(NC):
        cr = full(vr[i:i+1] * GAIN)
        ci = full(vi[i:i+1] * GAIN)
        comps.append((cr, ci))
        if i == NC - 1:
            break
        d = picks - picks[i:i+1]
        a = jnp.abs(d)
        alo, ahi = a & 127, a >> 7
        rr, ri = zero, zero
        for h in range(16):
            here = ahi == h
            rr = jnp.where(here, gather(full(spread[0, h:h+1, :]), alo), rr)
            ri = jnp.where(here, gather(full(spread[1, h:h+1, :]), alo), ri)
        ri = jnp.where(d < 0, -ri, ri)
        vr = vr - (cr * rr - ci * ri)
        vi = vi - (cr * ri + ci * rr)

    def model(pair, _):
        real, imag = [], []
        for part in range(2):
            g = pair * 2 + part
            q, u = joint[0, g], joint[1, g]
            mr, mi = zero, zero
            for j in range(NC):
                c, s = ec[g * NC + j], es[g * NC + j]
                cr, ci = comps[j]
                mr = mr + (cr * c - ci * s)
                mi = mi + (cr * s + ci * c)
            real.append(q - mr)
            imag.append(u - mi)
        out_ref[pl.ds(pl.multiple_of(pair * 16, 16), 16), :] = jnp.concatenate(real, axis=0).astype(jnp.bfloat16)
        out_ref[pl.ds(pl.multiple_of(chans + pair * 16, 16), 16), :] = jnp.concatenate(imag, axis=0).astype(jnp.bfloat16)
        return 0

    lax.fori_loop(0, groups // 2, model, 0)


def island_kernel(chans, stokes_ref, row_ref, peaks_ref, owner_ref, w_ref, out_ref, kt_ref, got_ref, last_ref,
                  raw, data, res, w, fit, sent, t, near, spread, kt, ck, sk, peaks, joint_peaks, oh, e4, ec, es, joint, chosen,
                  own, sa, ra, sn, rn, sf, rf, so, ow, op, sw, rw, sc, rc, sd, rd, od, ok):
    count, skies = lax.axis_size("freq"), lax.axis_size("sky")
    me = lax.axis_index("freq")
    sky = lax.axis_index("sky")
    x, z, core = sky // 8, sky // 2 % 4, sky % 2
    rows = stokes_ref.shape[2]
    tiles = stokes_ref.shape[3] // (count * 128)
    chunks = rows * tiles
    halfway = chunks // 2
    local = stokes_ref.shape[1]
    half = chans
    left, right, far = [lax.rem(me + k, count) for k in (count - 1, 1, 2)]

    def at_x(k):
        return {"sky": lax.rem(x + k, 4) * 8 + z * 2 + core}

    def at_z(k):
        return {"sky": x * 8 + lax.rem(z + k, 4) * 2 + core}

    other = {"sky": sky + 1 - 2 * core}

    barrier = pltpu.get_barrier_semaphore()
    for k in range(1, 4):
        pl.semaphore_signal(barrier, inc=1, device_id={"freq": lax.rem(me + k, count)}, device_id_type=MESH)

    def greet(k, _):
        pl.semaphore_signal(barrier, inc=1, device_id={"sky": lax.rem(sky + k, skies)}, device_id_type=MESH)
        return 0

    lax.fori_loop(1, skies, greet, 0)
    pl.semaphore_wait(barrier, count + skies - 2)

    def columns(owner, tile):
        return pl.ds(pl.multiple_of((owner * tiles + tile) * 128, 128), 128)

    def part(tile, k):
        peer = lax.rem(me + k, count)
        return pltpu.make_async_remote_copy(
            src_ref=stokes_ref.at[:, :, :, columns(peer, tile)], dst_ref=raw.at[tile, me],
            send_sem=sa.at[tile, k], recv_sem=ra.at[tile, k], device_id={"freq": peer}, device_id_type=MESH)

    def arrived(tile, k):
        source = lax.rem(me + count - k, count)
        return pltpu.make_async_remote_copy(
            src_ref=stokes_ref.at[:, :, :, columns(me, tile)], dst_ref=raw.at[tile, source],
            send_sem=sa.at[tile, k], recv_sem=ra.at[tile, k], device_id={"freq": source}, device_id_type=MESH)

    def kept(tile):
        return pltpu.make_async_copy(stokes_ref.at[:, :, :, columns(me, tile)], raw.at[tile, me], own.at[tile])

    for tile in range(tiles):
        kept(tile).start()
        for k in (1, 3, 2):
            part(tile, k).start()
    mine = pl.ds(pl.multiple_of(me * (tiles * 128), 128), tiles * 128)
    pltpu.make_async_copy(peaks_ref.at[:, :, mine], peaks, op).start()
    pltpu.make_async_copy(w_ref.at[0], w.at[x, z, core], ow).start()
    pltpu.make_async_copy(w_ref.at[0], w.at[x, z, core], ow).wait()

    def w_first(h, k, source=None):
        along_x = h == 0
        lines = pl.ds(h * half, half)
        piece = w.at[x, z, core, lines]
        if source is not None:
            piece = w.at[lax.rem(x + 4 - k, 4), z, core, lines] if along_x else w.at[x, lax.rem(z + 4 - k, 4), core, lines]
        return pltpu.make_async_remote_copy(
            src_ref=piece, dst_ref=piece, send_sem=sw.at[0, h, k], recv_sem=rw.at[0, h, k],
            device_id=at_x(k) if along_x else at_z(k), device_id_type=MESH)

    def w_second(h, k, source=None):
        along_x = h == 1
        lines = pl.ds(h * half, half)
        back = k if source is not None else 4
        if along_x:
            piece = w.at[lax.rem(x + 4 - back + (4 if back == 4 else 0), 4), :, core, lines]
        else:
            piece = w.at[:, lax.rem(z + 4 - back + (4 if back == 4 else 0), 4), core, lines]
        return pltpu.make_async_remote_copy(
            src_ref=piece, dst_ref=piece, send_sem=sw.at[1, h, k], recv_sem=rw.at[1, h, k],
            device_id=at_x(k) if along_x else at_z(k), device_id_type=MESH)

    def w_third(which):
        piece = w.at[:, :, which]
        return pltpu.make_async_remote_copy(
            src_ref=piece, dst_ref=piece, send_sem=sc, recv_sem=rc, device_id=other, device_id_type=MESH)

    for h in range(2):
        for k in range(1, 4):
            w_first(h, k).start()

    def slot(o, _):
        first, second = jnp.int32(-1), jnp.int32(-1)
        for b in reversed(range(owner_ref.shape[0])):
            hit = owner_ref[b] == o
            second = jnp.where(hit, first, second)
            first = jnp.where(hit, b, first)
        chosen[o * 2] = first
        chosen[o * 2 + 1] = second
        return 0

    lax.fori_loop(0, skies, slot, 0)
    make_tables(chans, row_ref, t, near, spread)

    def to_neighbour(c, way, source):
        return pltpu.make_async_remote_copy(
            src_ref=res.at[source, c], dst_ref=res.at[source, c],
            send_sem=sn.at[c, way], recv_sem=rn.at[c, way],
            device_id={"freq": right if way == 0 else left}, device_id_type=MESH)

    def onward(c, way, source):
        piece = res.at[source, c, pl.ds(way * half, half)]
        return pltpu.make_async_remote_copy(
            src_ref=piece, dst_ref=piece, send_sem=sf.at[c, way], recv_sem=rf.at[c, way],
            device_id={"freq": right if way == 0 else left}, device_id_type=MESH)

    def keep(c, source):
        return pltpu.make_async_copy(res.at[source, c], out_ref.at[source, c], so.at[c, source])

    def relay(c):
        to_neighbour(c, 0, left).wait_recv()
        onward(c, 0, left).start()
        keep(c, left).start()
        to_neighbour(c, 1, right).wait_recv()
        onward(c, 1, right).start()
        keep(c, right).start()

    def fit_chunk(source, c):
        part, tile, pair = c // halfway, c // 2 % tiles, c % 2
        b = pair * (2 * count * tiles) + source * tiles + tile
        after = b + count * tiles
        o, p = owner_ref[b], owner_ref[after]
        both = jnp.concatenate([w[o >> 3, (o >> 1) & 3, o & 1], w[p >> 3, (p >> 1) & 3, p & 1]], axis=1)
        value = lax.dot_general(res[source, c], both, (((0,), (0,)), ((), ())), preferred_element_type=jnp.float32)
        terms = value.shape[1] // 2
        fit[part, b] = value[:64, :terms].astype(jnp.bfloat16)
        fit[part, after] = value[64:, terms:].astype(jnp.bfloat16)

    def fit_some(sources, first, last):
        def some(c, _):
            for source in sources:
                fit_chunk(source, c)
            return 0
        lax.fori_loop(first, last, some, 0)

    def fit_far(first, last):
        def some(c, _):
            onward(c, 0, far).wait_recv()
            onward(c, 1, far).wait_recv()
            keep(c, far).start()
            fit_chunk(far, c)
            return 0
        lax.fori_loop(first, last, some, 0)

    def result(k, source):
        peer = lax.rem(sky + k, skies)
        return pltpu.make_async_remote_copy(
            src_ref=sent.at[peer], dst_ref=got_ref.at[source],
            send_sem=sd.at[k], recv_sem=rd.at[k], device_id={"sky": peer}, device_id_type=MESH)

    def kept_result():
        return pltpu.make_async_copy(sent.at[sky], got_ref.at[sky], od)

    def fill_slots(part, slots):
        def fill(o, _):
            for rank in range(2):
                b = chosen[o * 2 + rank]
                value = fit[part, jnp.maximum(b, 0)]
                slots[o, rank] = jnp.where(b >= 0, value, jnp.zeros_like(value))
            return 0

        lax.fori_loop(0, skies, fill, 0)

    def send_results(first, last):
        def send(k, _):
            result(lax.rem(k * 13, skies), sky).start()
            return 0

        lax.fori_loop(first, last, send, 0)

    pltpu.make_async_copy(peaks_ref.at[:, :, mine], peaks, op).wait()

    def step(c, _):
        part, tile, pair = c // halfway, c // 2 % tiles, c % 2

        @pl.when((pair == 0) & (part == 0))
        def _():
            kept(tile).wait()
            for k in (1, 3, 2):
                arrived(tile, k).wait_recv()
            for source in range(count):
                for plane in range(2):
                    block = raw[tile, source, plane].reshape(local * rows, 128)
                    data[tile, plane, source * local * rows:(source + 1) * local * rows, :] = block.astype(jnp.float32)
            joint_peaks[tile] = peaks[:, :, pl.ds(pl.multiple_of(tile * 128, 128), 128)].reshape(NC * rows, 128)

        clean_tile(chans, pair, part, rows, data.at[tile], joint_peaks.at[tile], t, spread, res.at[me, c], oh, e4, ec, es, joint)
        to_neighbour(c, 0, me).start()
        to_neighbour(c, 1, me).start()
        keep(c, me).start()

        @pl.when(c >= LAG)
        def _():
            relay(c - LAG)

        @pl.when(c == 1)
        def _():
            for h in range(2):
                for k in range(1, 4):
                    w_first(h, k, True).wait_recv()
            for h in range(2):
                for k in range(1, 4):
                    w_second(h, k).start()
            make_synthesis(chans, row_ref, me * (kt.shape[0] // 2), kt, ck, sk)
            pltpu.make_async_copy(kt, kt_ref, ok).start()

        @pl.when(c == 4)
        def _():
            for h in range(2):
                for k in range(1, 4):
                    w_second(h, k, True).wait_recv()
            w_third(core).start()

        @pl.when(c == 5)
        def _():
            w_third(1 - core).wait_recv()
            fit_some((me,), 0, halfway)
            fit_some((left, right), 0, halfway - 1)

        @pl.when(c == 6)
        def _():
            fit_some((left, right), halfway - 1, halfway)
            fit_far(0, halfway)
            fill_slots(0, sent)
            kept_result().start()
            send_results(1, 8)

        @pl.when(c == 7)
        def _():
            send_results(8, 16)

        return 0

    lax.fori_loop(0, chunks, step, 0)
    relay(chunks - 2)
    send_results(16, 24)
    fit_some((me,), halfway, chunks)
    relay(chunks - 1)
    send_results(24, skies)
    fit_some((left, right), halfway, chunks)
    fit_far(halfway, chunks)
    fill_slots(1, last_ref)

    for tile in range(tiles):
        for k in (1, 3, 2):
            part(tile, k).wait_send()
    for h in range(2):
        for k in range(1, 4):
            w_first(h, k).wait_send()
            w_second(h, k).wait_send()
    w_third(core).wait_send()

    def finish(c, _):
        to_neighbour(c, 0, me).wait_send()
        to_neighbour(c, 1, me).wait_send()
        onward(c, 0, left).wait_send()
        onward(c, 1, right).wait_send()
        for source in (me, left, right, far):
            keep(c, source).wait()
        return 0

    lax.fori_loop(0, chunks, finish, 0)
    pltpu.make_async_copy(kt, kt_ref, ok).wait()
    kept_result().wait()

    def results(k, _):
        result(k, lax.rem(sky + skies - k, skies)).wait_recv()
        result(k, sky).wait_send()
        return 0

    lax.fori_loop(1, skies, results, 0)


def islands(stokes, lam2, peaks, owners, weights, freq_count, sky_count):
    chans, local, rows, columns = lam2.shape[0], stokes.shape[1], stokes.shape[2], stokes.shape[3]
    groups = chans // 8
    tiles = columns // (freq_count * 128)
    chunks = rows * tiles
    terms = weights.shape[2]
    depths = DEPTHS // freq_count
    dma = pltpu.SemaphoreType.DMA
    vmem = pl.BlockSpec(memory_space=pltpu.VMEM)
    smem = pl.BlockSpec(memory_space=pltpu.SMEM)
    hbm = pl.BlockSpec(memory_space=pl.ANY)
    f32, bf16 = jnp.float32, jnp.bfloat16
    return pl.pallas_call(
        functools.partial(island_kernel, chans),
        in_specs=[hbm, vmem, hbm, smem, hbm],
        out_specs=[hbm, hbm, hbm, vmem],
        out_shape=[
            jax.ShapeDtypeStruct((freq_count, chunks, 2 * chans, 128), bf16),
            jax.ShapeDtypeStruct((2 * depths, 2 * chans), bf16),
            jax.ShapeDtypeStruct((sky_count, 2, 64, terms), bf16),
            jax.ShapeDtypeStruct((sky_count, 2, 64, terms), bf16),
        ],
        scratch_shapes=[
            pltpu.VMEM((tiles, freq_count, 2, local, rows, 128), bf16),
            pltpu.VMEM((tiles, 2, chans * rows, 128), f32),
            pltpu.VMEM((freq_count, chunks, 2 * chans, 128), bf16),
            pltpu.VMEM((4, 4, 2, 2 * chans, terms), bf16),
            pltpu.VMEM((2, freq_count * chunks, 64, terms), bf16),
            pltpu.VMEM((sky_count, 2, 64, terms), bf16),
            pltpu.VMEM((4 * chans, 256), bf16),
            pltpu.VMEM((2, chans, 128), f32),
            pltpu.VMEM((2, 16, 128), f32),
            pltpu.VMEM((2 * depths, 2 * chans), bf16),
            pltpu.VMEM((LOW, 2 * chans), f32),
            pltpu.VMEM((LOW, 2 * chans), f32),
            pltpu.VMEM((NC, rows, tiles * 128), jnp.int32),
            pltpu.VMEM((tiles, NC * rows, 128), jnp.int32),
            pltpu.VMEM((256, NC * 128), bf16),
            pltpu.VMEM((4 * chans, NC * 128), f32),
            pltpu.VMEM((groups * NC, 8, 128), f32),
            pltpu.VMEM((groups * NC, 8, 128), f32),
            pltpu.VMEM((2, groups, 8, 128), f32),
            pltpu.SMEM((sky_count * 2,), jnp.int32),
            dma((tiles,)), dma((tiles, 4)), dma((tiles, 4)),
            dma((chunks, 2)), dma((chunks, 2)), dma((chunks, 2)), dma((chunks, 2)), dma((chunks, 4)),
            dma, dma, dma((2, 2, 4)), dma((2, 2, 4)), dma, dma,
            dma((sky_count,)), dma((sky_count,)), dma, dma,
        ],
        compiler_params=pltpu.CompilerParams(collective_id=0, has_side_effects=True, vmem_limit_bytes=60 << 20),
        cost_estimate=pl.CostEstimate(flops=6 << 32, bytes_accessed=24 << 20, transcendentals=0),
        name="islands",
    )(stokes, lam2, peaks, owners, weights)


def shards(stokes, lam2, peaks, island_owner, fit_matrix):
    freq_count, sky_count = lax.axis_size("freq"), lax.axis_size("sky")
    res, kt, early, late = islands(stokes, lam2, peaks, island_owner[:, 0], fit_matrix, freq_count, sky_count)
    late = lax.all_to_all(late, "sky", split_axis=0, concat_axis=0, tiled=True)
    coefficients = jnp.concatenate([early, late], axis=2)
    return fdf(kt, res, stokes.shape[2]), coefficients.astype(jnp.float32)[None]


def solution(mesh):
    in_specs = (
        P(None, "freq", "sky", None),
        P(),
        P(None, "sky", None),
        P("sky", None),
        P("sky", None, "freq"),
    )
    out_specs = (P(None, "freq", "sky", None), P("sky", None, None, None, "freq"))
    return jax.shard_map(shards, mesh=mesh, in_specs=in_specs, out_specs=out_specs, check_vma=False)
```

```python
import functools
import jax
import jax.numpy as jnp
from jax import lax
from jax.sharding import PartitionSpec as P
from jax.experimental import pallas as pl
from jax.experimental.pallas import tpu as pltpu

NC = 8
DEPTHS = 2048
STEP = 2.5
BLK = 128
LAG = 2
MESH = pl.DeviceIdType.MESH
GAIN = 0.3
LOW = 64

def gather(x, idx):
    return jnp.take_along_axis(x, idx, axis=1, mode="promise_in_bounds")


def full(row):
    return jnp.broadcast_to(row, (8, 128))


def make_tables(chans, row_ref, t, near, spread):
    mean = jnp.sum(row_ref[...].reshape(1, chans), axis=1, keepdims=True) / chans
    along = jnp.broadcast_to(row_ref[...].reshape(1, chans) - mean, (8, chans))
    place = lax.broadcasted_iota(jnp.int32, (8, chans), 1) - lax.broadcasted_iota(jnp.int32, (8, chans), 0)
    lane = lax.broadcasted_iota(jnp.int32, (8, 128), 1)
    low = lane < LOW
    depth = jnp.where(low, lane, (lane - LOW) * LOW - DEPTHS // 2).astype(jnp.float32) * STEP
    plain = lane.astype(jnp.float32) * STEP

    def rows(g, _):
        twice = 2.0 * jnp.sum(jnp.where(place == g * 8, along, 0.0), axis=1, keepdims=True)
        angle = twice * depth
        parts = []
        for mask in (low, ~low):
            for value in (jnp.cos(angle), jnp.sin(angle)):
                value = jnp.where(mask, value, 0.0)
                top = value.astype(jnp.bfloat16)
                parts.append(jnp.concatenate([top, (value - top.astype(jnp.float32)).astype(jnp.bfloat16)], axis=1))
        t[pl.ds(pl.multiple_of(g * 32, 32), 32), :] = jnp.concatenate(parts, axis=0)
        angle = twice * plain
        near[0, pl.ds(pl.multiple_of(g * 8, 8), 8), :] = jnp.cos(angle)
        near[1, pl.ds(pl.multiple_of(g * 8, 8), 8), :] = jnp.sin(angle)
        return 0

    lax.fori_loop(0, chans // 8, rows, 0)
    twice = 2.0 * (row_ref[...].reshape(1, chans) - mean)
    angle = twice * (lax.broadcasted_iota(jnp.int32, (16, chans), 0).astype(jnp.float32) * (128 * STEP))
    cosine, sine = jnp.cos(angle), jnp.sin(angle)
    dot = functools.partial(jnp.dot, precision=lax.Precision.HIGHEST, preferred_element_type=jnp.float32)
    spread[0] = (dot(cosine, near[0]) - dot(sine, near[1])) / chans
    spread[1] = -(dot(sine, near[0]) + dot(cosine, near[1])) / chans


def make_synthesis(chans, row_ref, first, kt, ck, sk):
    total = 2 * chans
    depths = kt.shape[0] // 2
    mean = jnp.sum(row_ref[...].reshape(1, chans), axis=1, keepdims=True) / chans
    twice = 2.0 * (row_ref[...].reshape(1, chans) - mean)
    twice = jnp.concatenate([twice, twice], axis=1)
    fine = twice * (lax.broadcasted_iota(jnp.int32, (LOW, total), 0).astype(jnp.float32) * STEP)
    ck[...] = jnp.cos(fine)
    sk[...] = jnp.sin(fine)
    steps = lax.broadcasted_iota(jnp.int32, (8, total), 0) * LOW + (first - DEPTHS // 2)
    coarse = twice * (steps.astype(jnp.float32) * STEP)
    cosine, sine = jnp.cos(coarse), jnp.sin(coarse)
    is_q = lax.broadcasted_iota(jnp.int32, (16, total), 1) < chans
    for h in range(depths // LOW):
        ch, sh = cosine[h:h+1], sine[h:h+1]
        for l in range(0, LOW, 16):
            cl, sl = ck[l:l+16, :], sk[l:l+16, :]
            c = (ch * cl - sh * sl) / chans
            s = (sh * cl + ch * sl) / chans
            at = h * LOW + l
            kt[at:at+16, :] = jnp.where(is_q, c, s).astype(jnp.bfloat16)
            kt[depths+at:depths+at+16, :] = jnp.where(is_q, -s, c).astype(jnp.bfloat16)


def fdf_kernel(k_ref, res_ref, out_ref, mixed):
    rows, depths = out_ref.shape[2], k_ref.shape[0]
    for pair in range(rows // 2):
        a, b = res_ref[0, 0, 0, pair], res_ref[0, 1, 0, pair]
        block = jnp.concatenate([a[:, :64], b[:, :64], a[:, 64:], b[:, 64:]], axis=1)
        for first in range(0, depths, 256):
            part = jnp.dot(k_ref[first:first + 256, :], block, preferred_element_type=jnp.float32)
            for row in range(2):
                mixed[pl.ds(first * rows + pair * 2 + row, 256, rows), :] = part[:, row * 128:(row + 1) * 128]
    out_ref[...] = mixed[...].astype(jnp.bfloat16).reshape(out_ref.shape)


def fdf(kt, res, rows):
    count, chunks, total, _ = res.shape
    tiles = chunks // rows
    depths = kt.shape[0]
    columns = count * tiles * 128
    return pl.pallas_call(
        fdf_kernel,
        grid=(count * tiles,),
        in_specs=[
            pl.BlockSpec((depths, total), lambda i: (0, 0)),
            pl.BlockSpec((1, 2, 1, rows // 2, total, 128), lambda i: (i // tiles, 0, i % tiles, 0, 0, 0)),
        ],
        out_specs=pl.BlockSpec((2, depths // 2, rows, 128), lambda i: (0, 0, 0, i)),
        out_shape=jax.ShapeDtypeStruct((2, depths // 2, rows, columns), jnp.bfloat16),
        scratch_shapes=[pltpu.VMEM((depths * rows, 128), jnp.float32)],
        compiler_params=pltpu.CompilerParams(vmem_limit_bytes=48 << 20),
        cost_estimate=pl.CostEstimate(flops=2 * depths * total * rows * columns, bytes_accessed=14 << 20, transcendentals=0),
        name="fdf",
    )(kt, res.reshape(count, 2, tiles, rows // 2, total, 128))


def clean_tile(chans, pair, half, rows, data, peaks, t, spread, out_ref, oh, e4, ec, es, joint):
    groups = chans // 8
    stays, moves = pair * 2 + half, pair * 2 + 1 - half
    here = (lax.broadcasted_iota(jnp.int32, (8, 128), 1) < 64) == (half == 0)

    def merged(ref, base):
        kept = ref[pl.ds(base + stays, 8, rows), :]
        moved = ref[pl.ds(base + moves, 8, rows), :]
        return jnp.where(here, kept, pltpu.roll(moved, 64, 1))

    picks = merged(peaks, 0)
    lo = picks & (LOW - 1)
    hi = (picks >> 6) + LOW
    index = lax.broadcasted_iota(jnp.int32, (128, 128), 0)
    for j in range(NC):
        cols = slice(j * 128, (j + 1) * 128)
        hot = ((index == lo[j:j+1]) | (index == hi[j:j+1])).astype(jnp.bfloat16)
        oh[0:128, cols] = hot
        oh[128:256, cols] = hot
    e4[...] = jnp.dot(t[...], oh[...], preferred_element_type=jnp.float32)

    def join(g, _):
        for k in range(6):
            joint[0, g * 6 + k] = merged(data.at[0], (g * 6 + k) * (8 * rows))
            joint[1, g * 6 + k] = merged(data.at[1], (g * 6 + k) * (8 * rows))
        return 0

    lax.fori_loop(0, groups // 6, join, 0)

    def peak(g, acc):
        q, u = joint[0, g], joint[1, g]
        base = pl.multiple_of(g * 32, 32)
        out = []
        for j in range(NC):
            cols = slice(j * 128, (j + 1) * 128)
            cl, sl = e4[pl.ds(base, 8), cols], e4[pl.ds(base + 8, 8), cols]
            ch, sh = e4[pl.ds(base + 16, 8), cols], e4[pl.ds(base + 24, 8), cols]
            c = ch * cl - sh * sl
            s = sh * cl + ch * sl
            ec[g * NC + j] = c
            es[g * NC + j] = s
            out.append((acc[j][0] + (q * c + u * s), acc[j][1] + (u * c - q * s)))
        return tuple(out)

    zero = jnp.zeros((8, 128), jnp.float32)
    acc = lax.fori_loop(0, groups, peak, tuple((zero, zero) for _ in range(NC)))
    scale = 1.0 / chans
    vr = jnp.concatenate([jnp.sum(a[0], axis=0, keepdims=True) for a in acc], axis=0) * scale
    vi = jnp.concatenate([jnp.sum(a[1], axis=0, keepdims=True) for a in acc], axis=0) * scale
    comps = []
    for i in range(NC):
        cr = full(vr[i:i+1] * GAIN)
        ci = full(vi[i:i+1] * GAIN)
        comps.append((cr, ci))
        if i == NC - 1:
            break
        d = picks - picks[i:i+1]
        a = jnp.abs(d)
        alo, ahi = a & 127, a >> 7
        rr, ri = zero, zero
        for h in range(16):
            here = ahi == h
            rr = jnp.where(here, gather(full(spread[0, h:h+1, :]), alo), rr)
            ri = jnp.where(here, gather(full(spread[1, h:h+1, :]), alo), ri)
        ri = jnp.where(d < 0, -ri, ri)
        vr = vr - (cr * rr - ci * ri)
        vi = vi - (cr * ri + ci * rr)

    def model(pair, _):
        real, imag = [], []
        for part in range(2):
            g = pair * 2 + part
            q, u = joint[0, g], joint[1, g]
            mr, mi = zero, zero
            for j in range(NC):
                c, s = ec[g * NC + j], es[g * NC + j]
                cr, ci = comps[j]
                mr = mr + (cr * c - ci * s)
                mi = mi + (cr * s + ci * c)
            real.append(q - mr)
            imag.append(u - mi)
        out_ref[pl.ds(pl.multiple_of(pair * 16, 16), 16), :] = jnp.concatenate(real, axis=0).astype(jnp.bfloat16)
        out_ref[pl.ds(pl.multiple_of(chans + pair * 16, 16), 16), :] = jnp.concatenate(imag, axis=0).astype(jnp.bfloat16)
        return 0

    lax.fori_loop(0, groups // 2, model, 0)


def island_kernel(chans, stokes_ref, row_ref, peaks_ref, owner_ref, w_ref, out_ref, kt_ref, got_ref, last_ref,
                  raw, data, res, w, fit, sent, t, near, spread, kt, ck, sk, peaks, joint_peaks, oh, e4, ec, es, joint, chosen,
                  own, sa, ra, sn, rn, sf, rf, so, ow, op, sw, rw, sc, rc, sd, rd, od, ok):
    count, skies = lax.axis_size("freq"), lax.axis_size("sky")
    me = lax.axis_index("freq")
    sky = lax.axis_index("sky")
    x, z, core = sky // 8, sky // 2 % 4, sky % 2
    rows = stokes_ref.shape[2]
    tiles = stokes_ref.shape[3] // (count * 128)
    chunks = rows * tiles
    halfway = chunks // 2
    local = stokes_ref.shape[1]
    half = chans
    left, right, far = [lax.rem(me + k, count) for k in (count - 1, 1, 2)]

    def at_x(k):
        return {"sky": lax.rem(x + k, 4) * 8 + z * 2 + core}

    def at_z(k):
        return {"sky": x * 8 + lax.rem(z + k, 4) * 2 + core}

    other = {"sky": sky + 1 - 2 * core}

    barrier = pltpu.get_barrier_semaphore()
    for k in range(1, 4):
        pl.semaphore_signal(barrier, inc=1, device_id={"freq": lax.rem(me + k, count)}, device_id_type=MESH)

    def greet(k, _):
        pl.semaphore_signal(barrier, inc=1, device_id={"sky": lax.rem(sky + k, skies)}, device_id_type=MESH)
        return 0

    lax.fori_loop(1, skies, greet, 0)
    pl.semaphore_wait(barrier, count + skies - 2)

    def columns(owner, tile):
        return pl.ds(pl.multiple_of((owner * tiles + tile) * 128, 128), 128)

    def part(tile, k):
        peer = lax.rem(me + k, count)
        return pltpu.make_async_remote_copy(
            src_ref=stokes_ref.at[:, :, :, columns(peer, tile)], dst_ref=raw.at[tile, me],
            send_sem=sa.at[tile, k], recv_sem=ra.at[tile, k], device_id={"freq": peer}, device_id_type=MESH)

    def arrived(tile, k):
        source = lax.rem(me + count - k, count)
        return pltpu.make_async_remote_copy(
            src_ref=stokes_ref.at[:, :, :, columns(me, tile)], dst_ref=raw.at[tile, source],
            send_sem=sa.at[tile, k], recv_sem=ra.at[tile, k], device_id={"freq": source}, device_id_type=MESH)

    def kept(tile):
        return pltpu.make_async_copy(stokes_ref.at[:, :, :, columns(me, tile)], raw.at[tile, me], own.at[tile])

    for tile in range(tiles):
        kept(tile).start()
        for k in (2, 1, 3):
            part(tile, k).start()
    mine = pl.ds(pl.multiple_of(me * (tiles * 128), 128), tiles * 128)
    pltpu.make_async_copy(peaks_ref.at[:, :, mine], peaks, op).start()
    pltpu.make_async_copy(w_ref.at[0], w.at[x, z, core], ow).start()
    pltpu.make_async_copy(w_ref.at[0], w.at[x, z, core], ow).wait()

    def w_first(h, k, source=None):
        along_x = h == 0
        lines = pl.ds(h * half, half)
        piece = w.at[x, z, core, lines]
        if source is not None:
            piece = w.at[lax.rem(x + 4 - k, 4), z, core, lines] if along_x else w.at[x, lax.rem(z + 4 - k, 4), core, lines]
        return pltpu.make_async_remote_copy(
            src_ref=piece, dst_ref=piece, send_sem=sw.at[0, h, k], recv_sem=rw.at[0, h, k],
            device_id=at_x(k) if along_x else at_z(k), device_id_type=MESH)

    def w_second(h, k, source=None):
        along_x = h == 1
        lines = pl.ds(h * half, half)
        back = k if source is not None else 4
        if along_x:
            piece = w.at[lax.rem(x + 4 - back + (4 if back == 4 else 0), 4), :, core, lines]
        else:
            piece = w.at[:, lax.rem(z + 4 - back + (4 if back == 4 else 0), 4), core, lines]
        return pltpu.make_async_remote_copy(
            src_ref=piece, dst_ref=piece, send_sem=sw.at[1, h, k], recv_sem=rw.at[1, h, k],
            device_id=at_x(k) if along_x else at_z(k), device_id_type=MESH)

    def w_third(which):
        piece = w.at[:, :, which]
        return pltpu.make_async_remote_copy(
            src_ref=piece, dst_ref=piece, send_sem=sc, recv_sem=rc, device_id=other, device_id_type=MESH)

    for h in range(2):
        for k in range(1, 4):
            w_first(h, k).start()

    def slot(o, _):
        first, second = jnp.int32(-1), jnp.int32(-1)
        for b in reversed(range(owner_ref.shape[0])):
            hit = owner_ref[b] == o
            second = jnp.where(hit, first, second)
            first = jnp.where(hit, b, first)
        chosen[o * 2] = first
        chosen[o * 2 + 1] = second
        return 0

    lax.fori_loop(0, skies, slot, 0)
    make_tables(chans, row_ref, t, near, spread)

    def to_neighbour(c, way, source):
        return pltpu.make_async_remote_copy(
            src_ref=res.at[source, c], dst_ref=res.at[source, c],
            send_sem=sn.at[c, way], recv_sem=rn.at[c, way],
            device_id={"freq": right if way == 0 else left}, device_id_type=MESH)

    def onward(c, way, source):
        piece = res.at[source, c, pl.ds(way * half, half)]
        return pltpu.make_async_remote_copy(
            src_ref=piece, dst_ref=piece, send_sem=sf.at[c, way], recv_sem=rf.at[c, way],
            device_id={"freq": right if way == 0 else left}, device_id_type=MESH)

    def keep(c, source):
        return pltpu.make_async_copy(res.at[source, c], out_ref.at[source, c], so.at[c, source])

    def relay(c):
        to_neighbour(c, 0, left).wait_recv()
        onward(c, 0, left).start()
        keep(c, left).start()
        to_neighbour(c, 1, right).wait_recv()
        onward(c, 1, right).start()
        keep(c, right).start()

    def fit_chunk(source, c):
        part, tile, pair = c // halfway, c // 2 % tiles, c % 2
        b = pair * (2 * count * tiles) + source * tiles + tile
        after = b + count * tiles
        o, p = owner_ref[b], owner_ref[after]
        both = jnp.concatenate([w[o >> 3, (o >> 1) & 3, o & 1], w[p >> 3, (p >> 1) & 3, p & 1]], axis=1)
        value = lax.dot_general(res[source, c], both, (((0,), (0,)), ((), ())), preferred_element_type=jnp.float32)
        terms = value.shape[1] // 2
        fit[part, b] = value[:64, :terms].astype(jnp.bfloat16)
        fit[part, after] = value[64:, terms:].astype(jnp.bfloat16)

    def fit_some(sources, first, last):
        def some(c, _):
            for source in sources:
                fit_chunk(source, c)
            return 0
        lax.fori_loop(first, last, some, 0)

    def fit_far(first, last):
        def some(c, _):
            onward(c, 0, far).wait_recv()
            onward(c, 1, far).wait_recv()
            keep(c, far).start()
            fit_chunk(far, c)
            return 0
        lax.fori_loop(first, last, some, 0)

    def result(k, source):
        peer = lax.rem(sky + k, skies)
        return pltpu.make_async_remote_copy(
            src_ref=sent.at[peer], dst_ref=got_ref.at[source],
            send_sem=sd.at[k], recv_sem=rd.at[k], device_id={"sky": peer}, device_id_type=MESH)

    def kept_result():
        return pltpu.make_async_copy(sent.at[sky], got_ref.at[sky], od)

    def fill_slots(part, slots):
        def fill(o, _):
            for rank in range(2):
                b = chosen[o * 2 + rank]
                value = fit[part, jnp.maximum(b, 0)]
                slots[o, rank] = jnp.where(b >= 0, value, jnp.zeros_like(value))
            return 0

        lax.fori_loop(0, skies, fill, 0)

    def send_results(first, last):
        def send(k, _):
            result(lax.rem(k * 13, skies), sky).start()
            return 0

        lax.fori_loop(first, last, send, 0)

    pltpu.make_async_copy(peaks_ref.at[:, :, mine], peaks, op).wait()

    def step(c, _):
        part, tile, pair = c // halfway, c // 2 % tiles, c % 2

        @pl.when((pair == 0) & (part == 0))
        def _():
            kept(tile).wait()
            for k in (1, 3, 2):
                arrived(tile, k).wait_recv()
            for source in range(count):
                for plane in range(2):
                    block = raw[tile, source, plane].reshape(local * rows, 128)
                    data[tile, plane, source * local * rows:(source + 1) * local * rows, :] = block.astype(jnp.float32)
            joint_peaks[tile] = peaks[:, :, pl.ds(pl.multiple_of(tile * 128, 128), 128)].reshape(NC * rows, 128)

        clean_tile(chans, pair, part, rows, data.at[tile], joint_peaks.at[tile], t, spread, res.at[me, c], oh, e4, ec, es, joint)
        to_neighbour(c, 0, me).start()
        to_neighbour(c, 1, me).start()
        keep(c, me).start()

        @pl.when(c >= LAG)
        def _():
            relay(c - LAG)

        @pl.when(c == 1)
        def _():
            for h in range(2):
                for k in range(1, 4):
                    w_first(h, k, True).wait_recv()
            for h in range(2):
                for k in range(1, 4):
                    w_second(h, k).start()
            make_synthesis(chans, row_ref, me * (kt.shape[0] // 2), kt, ck, sk)
            pltpu.make_async_copy(kt, kt_ref, ok).start()

        @pl.when(c == 4)
        def _():
            for h in range(2):
                for k in range(1, 4):
                    w_second(h, k, True).wait_recv()
            w_third(core).start()

        @pl.when(c == 5)
        def _():
            w_third(1 - core).wait_recv()
            fit_some((me,), 0, halfway)
            fit_some((left, right), 0, halfway - 1)

        @pl.when(c == 6)
        def _():
            fit_some((left, right), halfway - 1, halfway)
            fit_far(0, halfway)
            fill_slots(0, sent)
            kept_result().start()
            send_results(1, 8)

        @pl.when(c == 7)
        def _():
            send_results(8, 16)

        return 0

    lax.fori_loop(0, chunks, step, 0)
    relay(chunks - 2)
    send_results(16, 24)
    fit_some((me,), halfway, chunks)
    relay(chunks - 1)
    send_results(24, skies)
    fit_some((left, right), halfway, chunks)
    fit_far(halfway, chunks)
    fill_slots(1, last_ref)

    for tile in range(tiles):
        for k in (1, 3, 2):
            part(tile, k).wait_send()
    for h in range(2):
        for k in range(1, 4):
            w_first(h, k).wait_send()
            w_second(h, k).wait_send()
    w_third(core).wait_send()

    def finish(c, _):
        to_neighbour(c, 0, me).wait_send()
        to_neighbour(c, 1, me).wait_send()
        onward(c, 0, left).wait_send()
        onward(c, 1, right).wait_send()
        for source in (me, left, right, far):
            keep(c, source).wait()
        return 0

    lax.fori_loop(0, chunks, finish, 0)
    pltpu.make_async_copy(kt, kt_ref, ok).wait()
    kept_result().wait()

    def results(k, _):
        result(k, lax.rem(sky + skies - k, skies)).wait_recv()
        result(k, sky).wait_send()
        return 0

    lax.fori_loop(1, skies, results, 0)


def islands(stokes, lam2, peaks, owners, weights, freq_count, sky_count):
    chans, local, rows, columns = lam2.shape[0], stokes.shape[1], stokes.shape[2], stokes.shape[3]
    groups = chans // 8
    tiles = columns // (freq_count * 128)
    chunks = rows * tiles
    terms = weights.shape[2]
    depths = DEPTHS // freq_count
    dma = pltpu.SemaphoreType.DMA
    vmem = pl.BlockSpec(memory_space=pltpu.VMEM)
    smem = pl.BlockSpec(memory_space=pltpu.SMEM)
    hbm = pl.BlockSpec(memory_space=pl.ANY)
    f32, bf16 = jnp.float32, jnp.bfloat16
    return pl.pallas_call(
        functools.partial(island_kernel, chans),
        in_specs=[hbm, vmem, hbm, smem, hbm],
        out_specs=[hbm, hbm, hbm, vmem],
        out_shape=[
            jax.ShapeDtypeStruct((freq_count, chunks, 2 * chans, 128), bf16),
            jax.ShapeDtypeStruct((2 * depths, 2 * chans), bf16),
            jax.ShapeDtypeStruct((sky_count, 2, 64, terms), bf16),
            jax.ShapeDtypeStruct((sky_count, 2, 64, terms), bf16),
        ],
        scratch_shapes=[
            pltpu.VMEM((tiles, freq_count, 2, local, rows, 128), bf16),
            pltpu.VMEM((tiles, 2, chans * rows, 128), f32),
            pltpu.VMEM((freq_count, chunks, 2 * chans, 128), bf16),
            pltpu.VMEM((4, 4, 2, 2 * chans, terms), bf16),
            pltpu.VMEM((2, freq_count * chunks, 64, terms), bf16),
            pltpu.VMEM((sky_count, 2, 64, terms), bf16),
            pltpu.VMEM((4 * chans, 256), bf16),
            pltpu.VMEM((2, chans, 128), f32),
            pltpu.VMEM((2, 16, 128), f32),
            pltpu.VMEM((2 * depths, 2 * chans), bf16),
            pltpu.VMEM((LOW, 2 * chans), f32),
            pltpu.VMEM((LOW, 2 * chans), f32),
            pltpu.VMEM((NC, rows, tiles * 128), jnp.int32),
            pltpu.VMEM((tiles, NC * rows, 128), jnp.int32),
            pltpu.VMEM((256, NC * 128), bf16),
            pltpu.VMEM((4 * chans, NC * 128), f32),
            pltpu.VMEM((groups * NC, 8, 128), f32),
            pltpu.VMEM((groups * NC, 8, 128), f32),
            pltpu.VMEM((2, groups, 8, 128), f32),
            pltpu.SMEM((sky_count * 2,), jnp.int32),
            dma((tiles,)), dma((tiles, 4)), dma((tiles, 4)),
            dma((chunks, 2)), dma((chunks, 2)), dma((chunks, 2)), dma((chunks, 2)), dma((chunks, 4)),
            dma, dma, dma((2, 2, 4)), dma((2, 2, 4)), dma, dma,
            dma((sky_count,)), dma((sky_count,)), dma, dma,
        ],
        compiler_params=pltpu.CompilerParams(collective_id=0, has_side_effects=True, vmem_limit_bytes=60 << 20),
        cost_estimate=pl.CostEstimate(flops=6 << 32, bytes_accessed=24 << 20, transcendentals=0),
        name="islands",
    )(stokes, lam2, peaks, owners, weights)


def shards(stokes, lam2, peaks, island_owner, fit_matrix):
    freq_count, sky_count = lax.axis_size("freq"), lax.axis_size("sky")
    res, kt, early, late = islands(stokes, lam2, peaks, island_owner[:, 0], fit_matrix, freq_count, sky_count)
    late = lax.all_to_all(late, "sky", split_axis=0, concat_axis=0, tiled=True)
    coefficients = jnp.concatenate([early, late], axis=2)
    return fdf(kt, res, stokes.shape[2]), coefficients.astype(jnp.float32)[None]


def solution(mesh):
    in_specs = (
        P(None, "freq", "sky", None),
        P(),
        P(None, "sky", None),
        P("sky", None),
        P("sky", None, "freq"),
    )
    out_specs = (P(None, "freq", "sky", None), P("sky", None, None, None, "freq"))
    return jax.shard_map(shards, mesh=mesh, in_specs=in_specs, out_specs=out_specs, check_vma=False)
```
